512 devices in a mesh: ctx: 64 (over z, y), kv: 8 (over x, core).
Axes of the slice: x: 4, y: 8, z: 8, core: 2. Of those that a mesh axis runs over, the one named last changes fastest.
Arguments:
- hidden: bfloat16 [2, 8, 8192], P(None, None, 'ctx'), may hold values from -6 to 6
- w_qkv: bfloat16 [8192, 10240], P('ctx', 'kv'), may hold values from -0.0625 to 0.0625
- w_out: bfloat16 [8192, 8192], P('kv', 'ctx'), may hold values from -0.5 to 0.5
- key_pages: bfloat16 [8, 2048, 16, 1024], P(None, 'ctx', None, 'kv'), may hold values from -320 to 320
- value_pages: bfloat16 [8, 2048, 16, 1024], P(None, 'ctx', None, 'kv'), may hold values from -6 to 6
- ctx_len: int32 [8], replicated, may hold values from 4096 to 32768, as said below
- selected: int32 [2, 8, 8, 256], P(None, None, 'kv'), may hold values from 0 to 2047, as said below
- tail_keys: bfloat16 [4096, 16, 1024], P('ctx', None, 'kv'), may hold values from -8 to 8
- tail_values: bfloat16 [4096, 16, 1024], P('ctx', None, 'kv'), may hold values from -6 to 6
- tail_count: int32 [8], replicated, may hold values from 1 to 1024, 4096 in all
- tail_dest: int32 [4096, 1], replicated, may hold values from 0 to 63; in each aligned block of 64 rows (0 to 63, 64 to 127, ...) at most 2 rows name the same one
Outputs:
- mixed: bfloat16 [2, 8, 8192], P(None, None, 'ctx')
- stored_keys: bfloat16 [8192, 16, 1024], P('ctx', None, 'kv')
- stored_values: bfloat16 [8192, 16, 1024], P('ctx', None, 'kv')
- stored_bounds: bfloat16 [8192, 2, 1024], P('ctx', None, 'kv')
The draws below stay inside these ranges and needn't reach their ends.
Inputs may be any that keep to these rules, and one draw needn't show every extreme that they name: `ctx_len`: some row has exactly 32768 tokens. `selected`: 256 different page numbers for each step, row and key-value head, each below ceil(ctx_len of the row / 16). `tail_count`: the counts add up to 4096; the largest is exactly 1024. `tail_dest`: among the 64 tail pages of one device, at most 2 name one owner, a bound that some block reaches.
All inputs are finite; a program needn't handle non-finite values.
Results may differ from the reference program's by a relative error of at most 0.012.
The reference program's roundings to bfloat16 on the way count: a program that leaves them out, or rounds other values in their place, can miss the bound.
Values may be sent and summed in bfloat16 or wider, within the bound.
A program may use at most 64 MiB of HBM per device.

```python
import math
import jax
import jax.numpy as jnp
import numpy as np
from jax import lax

D = 8192
HQ = 64
KVH = 8
HD = 128
GROUP = 8
ROWS = 8
STEPS = 2
PAGE = 16
PAGES_DEV = 32
SEL_DEV = 4
PAIR = 2
OUT_DEV = 64
PAGES_ROW = 2048
SELK = 256
TAIL_TOTAL = 4096
N_CTX = 64


def context_lengths(key):
    shortest = SEL_DEV * N_CTX * PAGE
    longest = PAGES_DEV * N_CTX * PAGE
    first_key, second_key = jax.random.split(key)
    drawn = jax.random.randint(first_key, (ROWS,), shortest, longest + 1)
    longest_row = jax.random.randint(second_key, (), 0, ROWS)
    return jnp.where(jnp.arange(ROWS) == longest_row, longest, drawn).astype(jnp.int32)


def draw_ctx_len(key, part):
    return context_lengths(key)


def draw_selected(key, part):
    lengths = context_lengths(key)
    key = jax.random.fold_in(key, 7)
    total_pages = PAGES_DEV * N_CTX
    live_pages = (lengths + PAGE - 1) // PAGE
    ranking = jax.random.randint(key, (STEPS, ROWS, KVH, total_pages), 0, 65536)
    page_ids = jnp.arange(total_pages, dtype=jnp.int32)
    ranking = ranking * total_pages + page_ids
    ranking = jnp.where(page_ids[None, None, None, :] < live_pages[None, :, None, None], ranking, -1 - page_ids)
    return lax.top_k(ranking, SELK)[1].astype(jnp.int32)


def draw_key_pages(key, part):
    key = jax.random.fold_in(key, 11)
    first_key = jax.random.fold_in(key, 0)
    base = jax.random.normal(first_key, (ROWS, PAGES_DEV * N_CTX, PAGE, KVH, HD), jnp.float32)
    base = jnp.clip(base, -6.0, 6.0) * 1.5
    return base.reshape(ROWS, PAGES_DEV * N_CTX, PAGE, KVH * HD).astype(jnp.bfloat16)


def block_levels(key, dims, shards, low, top_value):
    gain, own = 1.0, jax.random.fold_in(key, 6)
    for dim, shards_of in shards:
        draws = jnp.exp(jax.random.uniform(jax.random.fold_in(own, dim), (shards_of,), jnp.float32, low / len(shards), top_value / len(shards)))
        gain = gain * jnp.repeat(draws, dims[dim] // shards_of).reshape([-1 if axis == dim else 1 for axis in range(len(dims))])
    return gain


def length_profile(number_of, total, reach, skew):
    portions = [(1 << 20) // math.isqrt(grade ** skew) + 1 for grade in range(2, number_of + 1)]
    spare, given = total - reach - (number_of - 1), [1] * (number_of - 1)
    while spare > 0:
        movable = [i for i in range(number_of - 1) if given[i] < reach]
        whole, remaining = sum([portions[i] for i in movable]), spare
        for i in movable:
            addition = min(reach - given[i], max(1, remaining * portions[i] // whole), spare)
            given[i] = given[i] + addition
            spare = spare - addition
    return np.array([reach] + given)


def uneven_parts(key, number_of, total, most, slope):
    if number_of == 2:
        one = jax.random.randint(key, (), max(1, total - most), min(most, total - 1) + 1)
        return jnp.stack([one, total - one])
    tallies = jnp.asarray(length_profile(number_of, total, most, slope), jnp.int32)
    twos = (number_of - 1) // 2
    source_of, taker = tallies[1:1 + 2 * twos:2], tallies[2:2 + 2 * twos:2]
    slack = jnp.minimum(source_of - 1, most - taker)
    passed = jax.random.randint(jax.random.fold_in(key, 1), (twos,), 0, 1 << 20) % (slack + 1)
    tallies = tallies.at[1:1 + 2 * twos:2].set(source_of - passed).at[2:2 + 2 * twos:2].set(taker + passed)
    return tallies[jax.random.permutation(jax.random.fold_in(key, 2), number_of)]


def deal_out(key, own, number, rows, number_of, top, bound, skew):
    order = jax.random.permutation(key, number_of)
    crowded, ordinary = shares(number_of, rows * top, bound, skew, True), shares(number_of, rows * top, bound, skew, False)
    places = jnp.arange(number_of)

    def named(sizes, rotation):
        used = int((sizes > 0).sum())
        fixed = max(1, used // 4)
        moved = fixed + (places - fixed + rotation * (used - fixed)) % max(1, number_of - fixed)
        return jnp.zeros((number_of,), jnp.int32).at[order[jnp.where(places < fixed, places, moved)]].set(jnp.asarray(sizes, jnp.int32))

    sizes = jnp.where(number % 4 == 0, named(crowded, number // 4), named(ordinary, number - number // 4 - 1))
    mixed = jax.random.permutation(jax.random.fold_in(own, 3), number_of)
    donor, receiver = mixed[0:number_of // 2 * 2:2], mixed[1:number_of // 2 * 2:2]
    slack = jnp.minimum(sizes[donor] - 1, bound - sizes[receiver]) // 2
    slack = jnp.where((donor == order[0]) | (receiver == order[0]) | (sizes[receiver] == 0), 0, jnp.maximum(slack, 0))
    moved = jax.random.randint(jax.random.fold_in(own, 4), (number_of // 2,), 0, 1 << 20) % (slack + 1)
    sizes = sizes.at[donor].add(-moved).at[receiver].add(moved)
    members = jnp.searchsorted(jnp.cumsum(sizes), jnp.arange(rows * top), side="right").astype(jnp.int32)
    table = members.reshape(top, rows).T
    table = table[jax.random.permutation(jax.random.fold_in(own, 1), rows)]
    rotation = jax.random.randint(jax.random.fold_in(own, 2), (rows, 1), 0, top)
    return jnp.take_along_axis(table, (jnp.arange(top)[None, :] + rotation) % top, axis=1)


def shares(amount, total, bound, slope, full):
    portions = [(1 << 20) // math.isqrt(grade ** slope) + 1 for grade in range(1, amount + 1)]
    largest = bound if full else min(bound, max(-(-total // amount), total * portions[0] // sum(portions)))
    least = 1 if total - largest >= amount - 1 else 0
    counts, surplus = [largest] + [least] * (amount - 1), total - largest - least * (amount - 1)
    while surplus > 0:
        movable = [i for i in range(1, amount) if counts[i] < largest] or [i for i in range(1, amount) if counts[i] < bound]
        pool, budget = sum([portions[i] for i in movable]), surplus
        for i in movable:
            more = min(bound - counts[i], max(1, budget * portions[i] // pool), surplus)
            counts[i] = counts[i] + more
            surplus = surplus - more
    return np.array(counts)


def normal_values(key, dims, width, limit, pieces=(), held_as=jnp.bfloat16):
    values = jax.random.normal(key, dims, jnp.float32) * width
    if len(pieces) > 0:
        values = block_levels(key, dims, pieces, -0.22, 0.18) * values
    return jnp.clip(values, min=-limit, max=limit).astype(held_as)


def setup_inputs(seed: int = 0) -> dict:
    keys = jax.random.split(jax.random.key(seed), 12)
    hidden = normal_values(keys[0], (STEPS, ROWS, D), 1.0, 6.0, ((2, 64),))
    w_qkv = normal_values(keys[1], (D, KVH * (GROUP + 2) * HD), D ** -0.5, 0.0625, ((0, 64), (1, 8)))
    w_out = normal_values(keys[2], (HQ * HD, D), (HQ * HD // 64) ** -0.5, 0.5, ((0, 8), (1, 64)))
    key_pages = draw_key_pages(jax.random.fold_in(keys[11], 71), 0)
    value_pages = normal_values(keys[4], (ROWS, PAGES_ROW, PAGE, KVH * HD), 1.0, 6.0, ((1, 64), (3, 8)))
    ctx_len = draw_ctx_len(jax.random.fold_in(keys[11], 71), 0)
    selected = draw_selected(jax.random.fold_in(keys[11], 71), 0)
    tail_keys = normal_values(keys[7], (TAIL_TOTAL, PAGE, KVH * HD), 1.5, 8.0, ((0, 64), (2, 8)))
    tail_values = normal_values(keys[8], (TAIL_TOTAL, PAGE, KVH * HD), 1.0, 6.0, ((0, 64), (2, 8)))
    tail_count = uneven_parts(keys[9], ROWS, TAIL_TOTAL, 2 * TAIL_TOTAL // ROWS, 2).astype(jnp.int32)
    tail_dest_keys = jax.random.split(jax.random.fold_in(keys[10], 1), TAIL_TOTAL // OUT_DEV)
    tail_dest_turns = jax.random.permutation(jax.random.fold_in(keys[10], 3), TAIL_TOTAL // OUT_DEV)
    tail_dest = jax.vmap(lambda own, number: deal_out(jax.random.fold_in(keys[10], 2), own, number, OUT_DEV, N_CTX, 1, PAIR, 2))(tail_dest_keys, tail_dest_turns).reshape((TAIL_TOTAL, 1))
    return dict(hidden=hidden, w_qkv=w_qkv, w_out=w_out, key_pages=key_pages, value_pages=value_pages, ctx_len=ctx_len, selected=selected, tail_keys=tail_keys, tail_values=tail_values, tail_count=tail_count, tail_dest=tail_dest)


def rounded(values):
    return lax.optimization_barrier(values.astype(jnp.bfloat16)).astype(jnp.float32)

def tail_rows(tail_count):
    row_ends = jnp.cumsum(tail_count)
    slot_ids = jnp.arange(OUT_DEV * N_CTX, dtype=jnp.int32)
    return lax.optimization_barrier(jnp.sum((slot_ids[:, None] >= row_ends[None, :]).astype(jnp.int32), axis=1))

def reference(hidden, w_qkv, w_out, key_pages, value_pages, ctx_len, selected, tail_keys, tail_values, tail_count, tail_dest):
    group_size = HQ // KVH
    score_scale = 1.0 / math.sqrt(HD)
    projected = jnp.dot(hidden.reshape(STEPS * ROWS, D), w_qkv, preferred_element_type=jnp.float32)
    projected = projected.astype(jnp.bfloat16).reshape(STEPS, ROWS, KVH, group_size + 2, HD)
    queries = projected[:, :, :, :group_size]
    new_keys = projected[:, :, :, group_size]
    new_values = projected[:, :, :, group_size + 1]
    page_rows = tail_rows(tail_count)
    row_ids = jnp.arange(ROWS, dtype=jnp.int32)
    tail_member = page_rows[None, :] == row_ids[:, None]
    causal = jnp.arange(STEPS)[:, None] >= jnp.arange(STEPS)[None, :]

    def one_head(head_index):
        head_query = lax.dynamic_index_in_dim(queries, head_index, 2, keepdims=False).astype(jnp.float32)
        own_key = lax.dynamic_index_in_dim(new_keys, head_index, 2, keepdims=False).astype(jnp.float32)
        own_value = lax.dynamic_index_in_dim(new_values, head_index, 2, keepdims=False).astype(jnp.float32)
        head_keys = lax.dynamic_slice_in_dim(key_pages, head_index * HD, HD, 3)
        head_values = lax.dynamic_slice_in_dim(value_pages, head_index * HD, HD, 3)
        chosen = lax.dynamic_index_in_dim(selected, head_index, 2, keepdims=False)
        picked_keys = head_keys[row_ids[None, :, None], chosen].astype(jnp.float32)
        picked_values = head_values[row_ids[None, :, None], chosen].astype(jnp.float32)
        positions = chosen[..., None] * PAGE + jnp.arange(PAGE, dtype=jnp.int32)
        resident_live = positions < ctx_len[None, :, None, None]
        resident_scores = jnp.einsum('srgd,srktd->srgkt', head_query, picked_keys) * score_scale
        resident_scores = jnp.where(resident_live[:, :, None], resident_scores, -jnp.inf)
        tail_head_keys = lax.dynamic_slice_in_dim(tail_keys, head_index * HD, HD, 2).astype(jnp.float32)
        tail_head_values = lax.dynamic_slice_in_dim(tail_values, head_index * HD, HD, 2).astype(jnp.float32)
        tail_scores = jnp.einsum('srgd,ptd->srgpt', head_query, tail_head_keys) * score_scale
        tail_scores = jnp.where(tail_member[None, :, None, :, None], tail_scores, -jnp.inf)
        own_scores = jnp.einsum('srgd,urd->srgu', head_query, own_key) * score_scale
        own_scores = jnp.where(causal[:, None, None, :], own_scores, -jnp.inf)
        row_peak = jnp.maximum(jnp.maximum(lax.optimization_barrier(jnp.max(resident_scores, axis=(3, 4))), lax.optimization_barrier(jnp.max(tail_scores, axis=(3, 4)))), lax.optimization_barrier(jnp.max(own_scores, axis=3)))
        resident_weights = jnp.exp(resident_scores - row_peak[..., None, None])
        tail_weights = jnp.exp(tail_scores - row_peak[..., None, None])
        own_weights = jnp.exp(own_scores - row_peak[..., None])
        totals = lax.optimization_barrier(jnp.sum(resident_weights, axis=(3, 4))) + lax.optimization_barrier(jnp.sum(tail_weights, axis=(3, 4))) + lax.optimization_barrier(jnp.sum(own_weights, axis=3))
        weighted = jnp.einsum('srgkt,srktd->srgd', rounded(resident_weights), picked_values)
        weighted = weighted + jnp.einsum('srgpt,ptd->srgd', rounded(tail_weights), tail_head_values)
        weighted = weighted + jnp.einsum('srgu,urd->srgd', rounded(own_weights), own_value)
        return weighted / totals[..., None]
    head_outputs = lax.map(one_head, jnp.arange(KVH, dtype=jnp.int32))
    attention = head_outputs.transpose(1, 2, 0, 3, 4).reshape(STEPS * ROWS, HQ * HD).astype(jnp.bfloat16)
    mixed = jnp.dot(attention, w_out, preferred_element_type=jnp.float32).astype(jnp.bfloat16).reshape(STEPS, ROWS, D)
    slot_ids = jnp.arange(OUT_DEV * N_CTX, dtype=jnp.int32)
    source = slot_ids // OUT_DEV
    owner_ids = tail_dest[:, 0]
    earlier = (source[:, None] == source[None, :]) & (owner_ids[:, None] == owner_ids[None, :]) & (slot_ids[None, :] < slot_ids[:, None])
    rank_ids = lax.optimization_barrier(jnp.sum(earlier.astype(jnp.int32), axis=1))
    place_ids = owner_ids * (N_CTX * PAIR) + source * PAIR + rank_ids
    stored_keys = jnp.zeros((N_CTX * N_CTX * PAIR, PAGE, KVH * HD), jnp.bfloat16).at[place_ids].set(tail_keys)
    stored_values = jnp.zeros((N_CTX * N_CTX * PAIR, PAGE, KVH * HD), jnp.bfloat16).at[place_ids].set(tail_values)
    bounds = jnp.stack([lax.optimization_barrier(jnp.min(tail_keys, axis=1)), lax.optimization_barrier(jnp.max(tail_keys, axis=1))], axis=1)
    stored_bounds = jnp.zeros((N_CTX * N_CTX * PAIR, 2, KVH * HD), jnp.bfloat16).at[place_ids].set(bounds)
    return (mixed, stored_keys, stored_values, stored_bounds)
```

```python
import functools
import math

import jax
import jax.numpy as jnp
from jax import lax
from jax.experimental import pallas as pl
from jax.experimental.pallas import tpu as pltpu
from jax.sharding import PartitionSpec as P

HD = 128
GROUP = 8
PAIR = 2
ROWS = 8
STEPS = 2
PAGE = 16
NZ = 8
QR = STEPS * GROUP
PIECE = 24
NEG = -1e30
MESH = pl.DeviceIdType.MESH
ORDER = (1, 7, 2, 6, 3, 5, 4, 0)
PACE = ((0, 1), (2, 3), (4, 5), (6, 7))


def nt(a, b):
    return lax.dot_general(a, b, (((1,), (1,)), ((), ())), preferred_element_type=jnp.float32)


def nn(a, b):
    return jnp.dot(a, b, preferred_element_type=jnp.float32)


def body(
    ny, nkv, out_here, pages_here,
    ctx_len, tail_count, hidden, w_qkv, w_out, keys, values, selected, tail_k, tail_v, dest,
    mixed, out_k, out_v, out_min, out_max,
    hid_v, wq_v, wo_v, k_v, v_v, sel_v, dest_v, tk_v, tv_v,
    part, ra1, a2s, ra2, qsend, qbuf, bias, bsend, rb1, b2s, rb2, asend, abuf, attf, csend, rc,
    stage, trecv, inv_v, inv_s,
    in_sem, send_sem, za_sem, ya_sem, zq_sem, zb_sem, yb_sem, zt_sem, kv_sem,
    tail_send, tail_recv, out_sem, inv_sem, ready,
):
    ctx = lax.axis_index("ctx")
    kv = lax.axis_index("kv")
    z = lax.div(ctx, ny)
    y = lax.rem(ctx, ny)
    n_ctx = NZ * ny
    score_scale = 1.0 / math.sqrt(HD)
    tokens = pages_here * PAGE
    tail_tokens = out_here * PAGE

    def z_peer(d):
        peer = lax.rem(z + d, NZ)
        return peer, (peer * ny + y, kv)

    def y_peer(d):
        peer = lax.rem(y + d, ny)
        return peer, (z * ny + peer, kv)

    def kv_peer(d):
        peer = lax.rem(kv + d, nkv)
        return peer, (ctx, peer)

    barrier = pltpu.get_barrier_semaphore()
    peers = NZ - 1 + ny - 1 + nkv - 1
    for count, peer_of in ((NZ, z_peer), (ny, y_peer), (nkv, kv_peer)):
        for d in range(1, count):
            pl.semaphore_signal(barrier, inc=1, device_id=peer_of(d)[1], device_id_type=MESH)

    first = lax.div(ctx * out_here, 128) * 128
    loads = [
        (hidden, hid_v),
        (w_qkv, wq_v),
        (dest.at[:, pl.ds(pl.multiple_of(first, 128), 128)], dest_v),
        (tail_k, tk_v.at[pl.ds(0, out_here)]),
        (tail_v, tv_v.at[pl.ds(0, out_here)]),
        (selected, sel_v),
        (keys, k_v),
        (values, v_v),
        (w_out, wo_v),
    ]
    loads = [pltpu.make_async_copy(a, b, in_sem.at[i]) for i, (a, b) in enumerate(loads)]
    for load in loads:
        load.start()

    tk_v[out_here] = jnp.zeros((PAGE, HD), jnp.bfloat16)
    tv_v[out_here] = jnp.zeros((PAGE, HD), jnp.bfloat16)
    loads[2].wait()
    offset = ctx * out_here - first
    sub = lax.broadcasted_iota(jnp.int32, (128, 128), 0)
    lane = lax.broadcasted_iota(jnp.int32, (128, 128), 1)
    lane_mine = (lane >= offset) & (lane < offset + out_here)
    sub_mine = (sub >= offset) & (sub < offset + out_here)
    dest_row = jnp.broadcast_to(dest_v[...], (128, 128))
    dest_col = jnp.sum(jnp.where(sub == lane, dest_row, 0), axis=1, keepdims=True)
    same = (dest_row == dest_col) & lane_mine & (lane < sub)
    rank_col = jnp.sum(jnp.where(same, 1, 0), axis=1, keepdims=True)
    target = dest_col * PAIR + rank_col
    hit = (lane == target) & sub_mine
    table = jnp.sum(jnp.where(hit, sub - offset - out_here, 0), axis=0, keepdims=True) + out_here
    inv_v[...] = jnp.broadcast_to(table, (8, 128))
    table_copy = pltpu.make_async_copy(inv_v, inv_s, inv_sem.at[0])
    table_copy.start()

    loads[0].wait()
    loads[1].wait()
    proj = nn(hid_v[...], wq_v[...])
    for j in range(GROUP + 2):
        for s in range(STEPS):
            at = s * GROUP + j if j < GROUP else QR + (j - GROUP) * STEPS + s
            part[pl.ds(at, ROWS, stride=PIECE), :] = proj[s * ROWS:(s + 1) * ROWS, j * HD:(j + 1) * HD]

    pl.semaphore_wait(barrier, peers)
    for d in range(1, ny):
        pl.semaphore_signal(ready, inc=1, device_id=y_peer(d)[1], device_id_type=MESH)

    def piece(i):
        return pl.ds(pl.multiple_of(i * PIECE, 8), PIECE)

    def q_rows(i):
        return pl.ds(pl.multiple_of(i * QR, QR), QR)

    def exchange(phase, count, peer_of, me, src, dst, recv):
        copies = []
        for d in range(1, count):
            peer, device = peer_of(d)
            copy = pltpu.make_async_remote_copy(
                src_ref=src(peer), dst_ref=dst(me), send_sem=send_sem.at[phase, d], recv_sem=recv.at[me],
                device_id=device, device_id_type=MESH,
            )
            copy.start()
            copies.append(copy)

        def wait():
            for d in range(1, count):
                peer, device = peer_of(d)
                pltpu.make_async_remote_copy(
                    src_ref=src(peer), dst_ref=dst(peer), send_sem=send_sem.at[phase, d], recv_sem=recv.at[peer],
                    device_id=device, device_id_type=MESH,
                ).wait_recv()

        return wait, copies

    sent = []

    def tail_block(distance, i):
        to_z = lax.rem(z + distance, NZ)
        to_y = lax.rem(y + i, ny)
        return pltpu.make_async_remote_copy(
            src_ref=stage.at[to_z * ny + to_y], dst_ref=trecv.at[ctx],
            send_sem=tail_send.at[distance], recv_sem=tail_recv.at[z],
            device_id=(to_z * ny + to_y, kv), device_id_type=MESH,
        )

    def tail_start(batch):
        distance = ORDER[batch]
        if distance == 0:
            pltpu.make_async_copy(stage.at[ctx], trecv.at[ctx], tail_recv.at[z]).start()

        def start(i, carry):
            tail_block(distance, i).start()
            return carry

        lax.fori_loop(1 if distance == 0 else 0, ny, start, 0)

    wait, copies = exchange(0, NZ, z_peer, z, lambda p: part.at[piece(p)], lambda m: ra1.at[m], za_sem)
    sent += copies
    ra1[z] = part[piece(z), :]

    loads[3].wait()
    loads[4].wait()
    table_copy.wait()

    def place(d, carry):
        for k in range(PAIR):
            page = inv_s[0, d * PAIR + k]
            stage[d, 0, k] = tk_v[page]
            stage[d, 1, k] = tv_v[page]
        return carry

    lax.fori_loop(0, n_ctx, place, 0)
    if ny > 1:
        pl.semaphore_wait(ready, ny - 1)
    for batch in PACE[0]:
        tail_start(batch)

    wait()
    a2s[...] = functools.reduce(lambda a, b: a + b, [ra1[i] for i in range(NZ)])
    wait, copies = exchange(1, ny, y_peer, y, lambda p: a2s, lambda m: ra2.at[m], ya_sem)
    sent += copies
    ra2[y] = a2s[...]
    for batch in PACE[1]:
        tail_start(batch)

    loads[5].wait()
    token = lax.broadcasted_iota(jnp.int32, (1, tokens), 1)
    page = lax.shift_right_logical(token, 4)
    for r in range(ROWS):
        inside = ctx * tokens + token < ctx_len[r]
        for s in range(STEPS):
            rel = sel_v[s, r] - ctx * pages_here
            bit = lax.shift_left(jnp.ones_like(rel), jnp.bitwise_and(rel, 15)).astype(jnp.float32)
            low = jnp.sum(jnp.where((rel >= 0) & (rel < 16), bit, 0.0), axis=1, keepdims=True).astype(jnp.int32)
            high = jnp.sum(jnp.where((rel >= 16) & (rel < 32), bit, 0.0), axis=1, keepdims=True).astype(jnp.int32)
            word = jnp.where(page < 16, low, high)
            live = jnp.bitwise_and(lax.shift_right_logical(word, jnp.bitwise_and(page, 15)), 1) == 1
            bias[pl.ds(r * STEPS + s, 1), :] = jnp.where(live & inside, 0.0, NEG)

    wait()
    total = functools.reduce(lambda a, b: a + b, [ra2[i] for i in range(ny)])
    rounded = total.astype(jnp.bfloat16)
    my_q = rounded[:QR]
    new_kv = rounded.astype(jnp.float32)[QR:QR + 2 * STEPS]
    qsend[...] = my_q
    wait, copies = exchange(2, NZ, z_peer, z, lambda p: qsend, lambda m: qbuf.at[q_rows(m)], zq_sem)
    sent += copies
    qbuf[q_rows(z), :] = my_q
    for batch in PACE[2]:
        tail_start(batch)

    tail_token = lax.broadcasted_iota(jnp.int32, (1, tail_tokens), 1)
    slot = lax.shift_right_logical(tail_token, 4) + ctx * out_here
    tail_row = jnp.zeros((1, tail_tokens), jnp.int32)
    end = 0
    for r in range(ROWS):
        end = end + tail_count[r]
        tail_row = tail_row + jnp.where(slot >= end, 1, 0)
    loads[6].wait()
    loads[7].wait()
    wait()

    q_all = qbuf[...]
    scores_t = nt(q_all, tk_v[pl.ds(0, out_here)].reshape(tail_tokens, HD)) * score_scale
    q_row = lax.shift_right_logical(lax.broadcasted_iota(jnp.int32, (ROWS * QR, tail_tokens), 0), 4)
    scores_t = jnp.where(q_row == tail_row, scores_t, NEG)
    peak_t = jnp.max(scores_t, axis=1, keepdims=True)
    scores_r, peaks = [], []
    for r in range(ROWS):
        masked = nt(q_all[r * QR:(r + 1) * QR], k_v[r]) * score_scale
        masked = jnp.concatenate([
            masked[s * GROUP:(s + 1) * GROUP] + bias[pl.ds(r * STEPS + s, 1), :] for s in range(STEPS)
        ], axis=0)
        scores_r.append(masked)
        peaks.append(jnp.maximum(jnp.max(masked, axis=1, keepdims=True), peak_t[r * QR:(r + 1) * QR]))
    weights_t = jnp.exp(scores_t - jnp.concatenate(peaks, axis=0))
    sums_t = jnp.sum(weights_t, axis=1, keepdims=True)
    out_t = nn(weights_t.astype(jnp.bfloat16), tv_v[pl.ds(0, out_here)].reshape(tail_tokens, HD))
    lane8 = lax.broadcasted_iota(jnp.int32, (8, HD), 1)

    def pack(m, l):
        return jnp.where(
            lane8 < 32, m[:8], jnp.where(lane8 < 64, m[8:], jnp.where(lane8 < 96, l[:8], l[8:]))
        )

    for r in range(ROWS):
        weights_r = jnp.exp(scores_r[r] - peaks[r])
        sums = jnp.sum(weights_r, axis=1, keepdims=True) + sums_t[r * QR:(r + 1) * QR]
        out_r = nn(weights_r.astype(jnp.bfloat16), v_v[r]) + out_t[r * QR:(r + 1) * QR]
        bsend[pl.ds(r * PIECE, QR), :] = out_r
        bsend[pl.ds(r * PIECE + QR, 8), :] = pack(peaks[r], sums)

    wait, copies = exchange(3, NZ, z_peer, z, lambda p: bsend.at[piece(p)], lambda m: rb1.at[m], zb_sem)
    sent += copies
    rb1[z] = bsend[piece(z), :]
    for batch in PACE[3]:
        tail_start(batch)

    q_f = my_q.astype(jnp.float32)
    own_scores = [
        jnp.sum(q_f * new_kv[u:u + 1], axis=1, keepdims=True) * score_scale for u in range(STEPS)
    ]
    step_of = lax.shift_right_logical(lax.broadcasted_iota(jnp.int32, (QR, 1), 0), 3)
    own_scores = [jnp.where(step_of >= u, own_scores[u], NEG) for u in range(STEPS)]

    def merge(ref, count):
        tiles = [ref[i, pl.ds(QR, 8), :] for i in range(count)]
        ms = [jnp.concatenate([t[:, 0:1], t[:, 32:33]], axis=0) for t in tiles]
        ls = [jnp.concatenate([t[:, 64:65], t[:, 96:97]], axis=0) for t in tiles]
        return ms, ls, [ref[i, pl.ds(0, QR), :] for i in range(count)]

    def combine(ms, ls, os):
        m = functools.reduce(jnp.maximum, ms)
        factors = [jnp.exp(a - m) for a in ms]
        l = functools.reduce(lambda a, b: a + b, [f * a for f, a in zip(factors, ls)])
        o = functools.reduce(lambda a, b: a + b, [f * a for f, a in zip(factors, os)])
        return m, l, o

    wait()
    m, l, o = combine(*merge(rb1, NZ))
    b2s[pl.ds(0, QR), :] = o
    b2s[pl.ds(QR, 8), :] = pack(m, l)
    wait, copies = exchange(4, ny, y_peer, y, lambda p: b2s, lambda m: rb2.at[m], yb_sem)
    sent += copies
    rb2[y] = b2s[...]
    wait()
    ms, ls, os = merge(rb2, ny)
    peak = functools.reduce(jnp.maximum, ms + own_scores)
    factors = [jnp.exp(a - peak) for a in ms]
    own = [jnp.exp(a - peak) for a in own_scores]
    l = functools.reduce(lambda a, b: a + b, [f * a for f, a in zip(factors, ls)] + own)
    o = functools.reduce(lambda a, b: a + b, [f * a for f, a in zip(factors, os)] + [
        w.astype(jnp.bfloat16).astype(jnp.float32) * new_kv[STEPS + u:STEPS + u + 1] for u, w in enumerate(own)
    ])
    att = (o / l).astype(jnp.bfloat16)
    asend[...] = att
    wait, copies = exchange(5, NZ, z_peer, z, lambda p: asend, lambda m: abuf.at[q_rows(m)], zt_sem)
    sent += copies
    abuf[q_rows(z), :] = att
    loads[8].wait()
    wait()
    attf[...] = abuf[...].astype(jnp.float32)
    att_all = jnp.concatenate([
        jnp.concatenate([attf[pl.ds(s * GROUP + g, ROWS, stride=QR), :] for s in range(STEPS)], axis=0)
        for g in range(GROUP)
    ], axis=1).astype(jnp.bfloat16)
    mine = nn(att_all, wo_v[...])
    csend[...] = mine
    wait, copies = exchange(6, nkv, kv_peer, kv, lambda p: csend, lambda m: rc.at[m], kv_sem)
    sent += copies
    rc[kv] = mine
    wait()
    mixed[...] = functools.reduce(lambda a, b: a + b, [rc[i] for i in range(nkv)]).astype(jnp.bfloat16)

    stores = []
    for batch, distance in enumerate(ORDER):
        from_z = lax.rem(z + NZ - distance, NZ)
        rows = pl.ds(from_z * ny, ny)
        pltpu.make_async_copy(trecv.at[rows], trecv.at[rows], tail_recv.at[from_z]).wait()
        for which, ref in enumerate((out_k, out_v)):
            store = pltpu.make_async_copy(trecv.at[rows, which], ref.at[rows], out_sem.at[batch, which])
            store.start()
            stores.append(store)
        pages = trecv[rows, 0].astype(jnp.float32).reshape(ny * PAIR, PAGE, HD)
        at = pl.ds(pl.multiple_of(from_z * (ny * PAIR), ny * PAIR), ny * PAIR)
        out_min[at, :] = jnp.min(pages, axis=1).astype(jnp.bfloat16)
        out_max[at, :] = jnp.max(pages, axis=1).astype(jnp.bfloat16)
    for store in stores:
        store.wait()
    for copy in sent:
        copy.wait_send()
    for distance in range(NZ):
        sent_rows = pl.ds(0, ny - 1 if distance == 0 else ny)
        if ny > 1 or distance > 0:
            pltpu.make_async_copy(stage.at[sent_rows], stage.at[sent_rows], tail_send.at[distance]).wait()


def on_device(
    hidden, w_qkv, w_out, key_pages, value_pages, ctx_len, selected,
    tail_keys, tail_values, tail_count, tail_dest,
):
    n_ctx = lax.axis_size("ctx")
    nkv = lax.axis_size("kv")
    ny = n_ctx // NZ
    pages_here = key_pages.shape[1]
    out_here = tail_keys.shape[0]
    tokens = pages_here * PAGE
    tail_tokens = out_here * PAGE
    bf, f32, i32 = jnp.bfloat16, jnp.float32, jnp.int32
    any_spec = pl.BlockSpec(memory_space=pl.ANY)
    smem = pl.BlockSpec(memory_space=pltpu.SMEM)
    vmem = pl.BlockSpec(memory_space=pltpu.VMEM)
    dma = pltpu.SemaphoreType.DMA
    mixed, out_k, out_v, low, high = pl.pallas_call(
        functools.partial(body, ny, nkv, out_here, pages_here),
        out_shape=(
            jax.ShapeDtypeStruct((STEPS * ROWS, HD), bf),
            jax.ShapeDtypeStruct((n_ctx, PAIR, PAGE, HD), bf),
            jax.ShapeDtypeStruct((n_ctx, PAIR, PAGE, HD), bf),
            jax.ShapeDtypeStruct((n_ctx * PAIR, HD), bf),
            jax.ShapeDtypeStruct((n_ctx * PAIR, HD), bf),
        ),
        in_specs=[smem, smem] + [any_spec] * 9,
        out_specs=(vmem, any_spec, any_spec, vmem, vmem),
        scratch_shapes=[
            pltpu.VMEM((STEPS * ROWS, HD), bf),
            pltpu.VMEM(w_qkv.shape, bf),
            pltpu.VMEM(w_out.shape, bf),
            pltpu.VMEM((ROWS, tokens, HD), bf),
            pltpu.VMEM((ROWS, tokens, HD), bf),
            pltpu.VMEM(selected.shape, i32),
            pltpu.VMEM((1, 128), i32),
            pltpu.VMEM((out_here + 1, PAGE, HD), bf),
            pltpu.VMEM((out_here + 1, PAGE, HD), bf),
            pltpu.VMEM((ROWS * PIECE, HD), f32),
            pltpu.VMEM((NZ, PIECE, HD), f32),
            pltpu.VMEM((PIECE, HD), f32),
            pltpu.VMEM((ny, PIECE, HD), f32),
            pltpu.VMEM((QR, HD), bf),
            pltpu.VMEM((ROWS * QR, HD), bf),
            pltpu.VMEM((ROWS * STEPS, tokens), f32),
            pltpu.VMEM((ROWS * PIECE, HD), f32),
            pltpu.VMEM((NZ, PIECE, HD), f32),
            pltpu.VMEM((PIECE, HD), f32),
            pltpu.VMEM((ny, PIECE, HD), f32),
            pltpu.VMEM((QR, HD), bf),
            pltpu.VMEM((ROWS * QR, HD), bf),
            pltpu.VMEM((ROWS * QR, HD), f32),
            pltpu.VMEM((STEPS * ROWS, HD), f32),
            pltpu.VMEM((nkv, STEPS * ROWS, HD), f32),
            pltpu.VMEM((n_ctx, 2, PAIR, PAGE, HD), bf),
            pltpu.VMEM((n_ctx, 2, PAIR, PAGE, HD), bf),
            pltpu.VMEM((8, 128), i32),
            pltpu.SMEM((8, 128), i32),
            dma((9,)),
            dma((7, 8)),
            dma((NZ,)),
            dma((ny,)),
            dma((NZ,)),
            dma((NZ,)),
            dma((ny,)),
            dma((NZ,)),
            dma((nkv,)),
            dma((NZ,)),
            dma((NZ,)),
            dma((NZ, 2)),
            dma((1,)),
            pltpu.SemaphoreType.REGULAR,
        ],
        compiler_params=pltpu.CompilerParams(
            collective_id=0, has_side_effects=True, vmem_limit_bytes=32 * 1024 * 1024
        ),
    )(
        ctx_len, tail_count, hidden.reshape(STEPS * ROWS, HD), w_qkv, w_out,
        key_pages.reshape(ROWS, tokens, HD), value_pages.reshape(ROWS, tokens, HD), selected,
        tail_keys, tail_values, tail_dest.T,
    )
    return (
        mixed.reshape(STEPS, ROWS, HD),
        out_k.reshape(n_ctx * PAIR, PAGE, HD),
        out_v.reshape(n_ctx * PAIR, PAGE, HD),
        jnp.stack([low, high], axis=1),
    )


def solution(mesh):
    placed = (
        P(None, None, "ctx"),
        P("ctx", "kv"),
        P("kv", "ctx"),
        P(None, "ctx", None, "kv"),
        P(None, "ctx", None, "kv"),
        P(),
        P(None, None, "kv", None),
        P("ctx", None, "kv"),
        P("ctx", None, "kv"),
        P(),
        P(),
    )
    return jax.shard_map(
        on_device,
        mesh=mesh,
        in_specs=placed,
        out_specs=(
            P(None, None, "ctx"),
            P("ctx", None, "kv"),
            P("ctx", None, "kv"),
            P("ctx", None, "kv"),
        ),
        check_vma=False,
    )
```

```python
import functools
import math

import jax
import jax.numpy as jnp
from jax import lax
from jax.experimental import pallas as pl
from jax.experimental.pallas import tpu as pltpu
from jax.sharding import PartitionSpec as P

HD = 128
GROUP = 8
PAIR = 2
ROWS = 8
STEPS = 2
PAGE = 16
NZ = 8
QR = STEPS * GROUP
PIECE = 24
NEG = -1e30
MESH = pl.DeviceIdType.MESH
SCHEDULE = (((0, 2),), ((1, 2),), ((0, 5),), ((1, 5),), ((3, 2),), ((2, 3),), ((2, 4), (3, 5)))


def far_first(count):
    return sorted(range(1, count), key=lambda d: (-min(d, count - d), d))


def nt(a, b):
    return lax.dot_general(a, b, (((1,), (1,)), ((), ())), preferred_element_type=jnp.float32)


def nn(a, b):
    return jnp.dot(a, b, preferred_element_type=jnp.float32)


def body(
    ny, nkv, out_here, pages_here,
    ctx_len, tail_count, hidden, w_qkv, w_out, keys, values, selected, tail_k, tail_v, dest,
    mixed, got_k, got_v,
    hid_v, wq_v, wo_v, k_v, v_v, sel_v, dest_v, tk_v, tv_v,
    part, ra1, a2s, ra2, qsend, qbuf, bias, bsend, rb1, b2s, rb2, asend, abuf, attf, csend, rc,
    stage_k, stage_v, mid_k, mid_v, inv_v, inv_s,
    in_sem, send_sem, za_sem, ya_sem, zq_sem, yb_sem, zb_sem, yt_sem, kv_sem,
    tail_send, tail_recv, inv_sem,
):
    ctx = lax.axis_index("ctx")
    kv = lax.axis_index("kv")
    z = lax.div(ctx, ny)
    y = lax.rem(ctx, ny)
    n_ctx = NZ * ny
    score_scale = 1.0 / math.sqrt(HD)
    tokens = pages_here * PAGE
    tail_tokens = out_here * PAGE

    def z_peer(d):
        peer = lax.rem(z + d, NZ)
        return peer, (peer * ny + y, kv)

    def y_peer(d):
        peer = lax.rem(y + d, ny)
        return peer, (z * ny + peer, kv)

    def kv_peer(d):
        peer = lax.rem(kv + d, nkv)
        return peer, (ctx, peer)

    barrier = pltpu.get_barrier_semaphore()
    peers = NZ - 1 + ny - 1 + nkv - 1
    for count, peer_of in ((NZ, z_peer), (ny, y_peer), (nkv, kv_peer)):
        for d in range(1, count):
            pl.semaphore_signal(barrier, inc=1, device_id=peer_of(d)[1], device_id_type=MESH)

    first = lax.div(ctx * out_here, 128) * 128
    loads = [
        (hidden, hid_v),
        (w_qkv, wq_v),
        (dest.at[:, pl.ds(pl.multiple_of(first, 128), 128)], dest_v),
        (tail_k, tk_v.at[pl.ds(0, out_here)]),
        (tail_v, tv_v.at[pl.ds(0, out_here)]),
        (selected, sel_v),
        (keys, k_v),
        (values, v_v),
        (w_out, wo_v),
    ]
    loads = [pltpu.make_async_copy(a, b, in_sem.at[i]) for i, (a, b) in enumerate(loads)]
    for load in loads:
        load.start()

    tk_v[out_here] = jnp.zeros((PAGE, HD), jnp.bfloat16)
    tv_v[out_here] = jnp.zeros((PAGE, HD), jnp.bfloat16)
    loads[2].wait()
    offset = ctx * out_here - first
    sub = lax.broadcasted_iota(jnp.int32, (128, 128), 0)
    lane = lax.broadcasted_iota(jnp.int32, (128, 128), 1)
    lane_mine = (lane >= offset) & (lane < offset + out_here)
    sub_mine = (sub >= offset) & (sub < offset + out_here)
    dest_row = jnp.broadcast_to(dest_v[...], (128, 128))
    dest_col = jnp.sum(jnp.where(sub == lane, dest_row, 0), axis=1, keepdims=True)
    same = (dest_row == dest_col) & lane_mine & (lane < sub)
    rank_col = jnp.sum(jnp.where(same, 1, 0), axis=1, keepdims=True)
    target = dest_col * PAIR + rank_col
    hit = (lane == target) & sub_mine
    table = jnp.sum(jnp.where(hit, sub - offset - out_here, 0), axis=0, keepdims=True) + out_here
    inv_v[...] = jnp.broadcast_to(table, (8, 128))
    table_copy = pltpu.make_async_copy(inv_v, inv_s, inv_sem.at[0])
    table_copy.start()

    loads[0].wait()
    loads[1].wait()
    proj = nn(hid_v[...], wq_v[...])
    for j in range(GROUP + 2):
        for s in range(STEPS):
            at = s * GROUP + j if j < GROUP else QR + (j - GROUP) * STEPS + s
            part[pl.ds(at, ROWS, stride=PIECE), :] = proj[s * ROWS:(s + 1) * ROWS, j * HD:(j + 1) * HD]

    pl.semaphore_wait(barrier, peers)

    def piece(i):
        return pl.ds(pl.multiple_of(i * PIECE, 8), PIECE)

    def q_rows(i):
        return pl.ds(pl.multiple_of(i * QR, QR), QR)

    def exchange(phase, count, peer_of, me, src, dst, recv):
        copies = []
        for d in range(1, count):
            peer, device = peer_of(d)
            copy = pltpu.make_async_remote_copy(
                src_ref=src(peer), dst_ref=dst(me), send_sem=send_sem.at[phase, d], recv_sem=recv.at[me],
                device_id=device, device_id_type=MESH,
            )
            copy.start()
            copies.append(copy)

        def wait():
            for d in range(1, count):
                peer, device = peer_of(d)
                pltpu.make_async_remote_copy(
                    src_ref=src(peer), dst_ref=dst(peer), send_sem=send_sem.at[phase, d], recv_sem=recv.at[peer],
                    device_id=device, device_id_type=MESH,
                ).wait_recv()

        return wait, copies

    sent = []

    tail_peer = (y_peer, z_peer, z_peer, y_peer)
    tail_order = (far_first(ny), far_first(NZ), far_first(NZ), far_first(ny))
    tail_src = (
        lambda p: stage_k.at[p], lambda p: stage_v.at[p], lambda p: mid_k.at[:, p], lambda p: mid_v.at[:, p],
    )
    tail_dst = (mid_k.at[y], mid_v.at[z], got_k.at[z], got_v.at[:, y])
    tail_me = (y, z, z, y)
    landing = (mid_k, mid_v, got_k, got_v)
    begun = [0, 0, 0, 0]

    def tail_start(phase):
        for kind, number in SCHEDULE[phase]:
            if begun[kind] == 0:
                if kind >= 2:
                    pltpu.make_async_copy(landing[kind - 2], landing[kind - 2], tail_recv.at[kind - 2]).wait()
                pltpu.make_async_copy(tail_src[kind](tail_me[kind]), tail_dst[kind], tail_recv.at[kind]).start()
            for d in tail_order[kind][begun[kind]:begun[kind] + number]:
                peer, device = tail_peer[kind](d)
                pltpu.make_async_remote_copy(
                    src_ref=tail_src[kind](peer), dst_ref=tail_dst[kind], send_sem=tail_send.at[kind],
                    recv_sem=tail_recv.at[kind], device_id=device, device_id_type=MESH,
                ).start()
            begun[kind] += number

    wait, copies = exchange(0, NZ, z_peer, z, lambda p: part.at[piece(p)], lambda m: ra1.at[m], za_sem)
    sent += copies
    ra1[z] = part[piece(z), :]

    loads[3].wait()
    loads[4].wait()
    table_copy.wait()

    def place(d, carry):
        to_z = lax.div(d, ny)
        to_y = lax.rem(d, ny)
        for k in range(PAIR):
            page = inv_s[0, d * PAIR + k]
            stage_k[to_y, to_z, k] = tk_v[page]
            stage_v[to_z, to_y, k] = tv_v[page]
        return carry

    lax.fori_loop(0, n_ctx, place, 0)
    tail_start(0)

    wait()
    a2s[...] = functools.reduce(lambda a, b: a + b, [ra1[i] for i in range(NZ)])
    wait, copies = exchange(1, ny, y_peer, y, lambda p: a2s, lambda m: ra2.at[m], ya_sem)
    sent += copies
    ra2[y] = a2s[...]
    tail_start(1)

    loads[5].wait()
    token = lax.broadcasted_iota(jnp.int32, (1, tokens), 1)
    page = lax.shift_right_logical(token, 4)
    for r in range(ROWS):
        inside = ctx * tokens + token < ctx_len[r]
        for s in range(STEPS):
            rel = sel_v[s, r] - ctx * pages_here
            bit = lax.shift_left(jnp.ones_like(rel), jnp.bitwise_and(rel, 15)).astype(jnp.float32)
            low = jnp.sum(jnp.where((rel >= 0) & (rel < 16), bit, 0.0), axis=1, keepdims=True).astype(jnp.int32)
            high = jnp.sum(jnp.where((rel >= 16) & (rel < 32), bit, 0.0), axis=1, keepdims=True).astype(jnp.int32)
            word = jnp.where(page < 16, low, high)
            live = jnp.bitwise_and(lax.shift_right_logical(word, jnp.bitwise_and(page, 15)), 1) == 1
            bias[pl.ds(r * STEPS + s, 1), :] = jnp.where(live & inside, 0.0, NEG)

    wait()
    total = functools.reduce(lambda a, b: a + b, [ra2[i] for i in range(ny)])
    rounded = total.astype(jnp.bfloat16)
    my_q = rounded[:QR]
    new_kv = rounded.astype(jnp.float32)[QR:QR + 2 * STEPS]
    qsend[...] = my_q
    wait, copies = exchange(2, NZ, z_peer, z, lambda p: qsend, lambda m: qbuf.at[q_rows(m)], zq_sem)
    sent += copies
    qbuf[q_rows(z), :] = my_q
    tail_start(2)

    tail_token = lax.broadcasted_iota(jnp.int32, (1, tail_tokens), 1)
    slot = lax.shift_right_logical(tail_token, 4) + ctx * out_here
    tail_row = jnp.zeros((1, tail_tokens), jnp.int32)
    end = 0
    for r in range(ROWS):
        end = end + tail_count[r]
        tail_row = tail_row + jnp.where(slot >= end, 1, 0)
    loads[6].wait()
    loads[7].wait()
    wait()

    q_all = qbuf[...]
    scores_t = nt(q_all, tk_v[pl.ds(0, out_here)].reshape(tail_tokens, HD)) * score_scale
    q_row = lax.shift_right_logical(lax.broadcasted_iota(jnp.int32, (ROWS * QR, tail_tokens), 0), 4)
    scores_t = jnp.where(q_row == tail_row, scores_t, NEG)
    peak_t = jnp.max(scores_t, axis=1, keepdims=True)
    scores_r, peaks = [], []
    for r in range(ROWS):
        masked = nt(q_all[r * QR:(r + 1) * QR], k_v[r]) * score_scale
        masked = jnp.concatenate([
            masked[s * GROUP:(s + 1) * GROUP] + bias[pl.ds(r * STEPS + s, 1), :] for s in range(STEPS)
        ], axis=0)
        scores_r.append(masked)
        peaks.append(jnp.maximum(jnp.max(masked, axis=1, keepdims=True), peak_t[r * QR:(r + 1) * QR]))
    weights_t = jnp.exp(scores_t - jnp.concatenate(peaks, axis=0))
    sums_t = jnp.sum(weights_t, axis=1, keepdims=True)
    out_t = nn(weights_t.astype(jnp.bfloat16), tv_v[pl.ds(0, out_here)].reshape(tail_tokens, HD))
    lane8 = lax.broadcasted_iota(jnp.int32, (8, HD), 1)

    def pack(m, l):
        return jnp.where(
            lane8 < 32, m[:8], jnp.where(lane8 < 64, m[8:], jnp.where(lane8 < 96, l[:8], l[8:]))
        )

    for r in range(ROWS):
        weights_r = jnp.exp(scores_r[r] - peaks[r])
        sums = jnp.sum(weights_r, axis=1, keepdims=True) + sums_t[r * QR:(r + 1) * QR]
        out_r = nn(weights_r.astype(jnp.bfloat16), v_v[r]) + out_t[r * QR:(r + 1) * QR]
        bsend[pl.ds(r * PIECE, QR), :] = out_r
        bsend[pl.ds(r * PIECE + QR, 8), :] = pack(peaks[r], sums)

    wait, copies = exchange(3, ny, y_peer, y, lambda p: bsend.at[piece(p)], lambda m: rb1.at[m], yb_sem)
    sent += copies
    rb1[y] = bsend[piece(y), :]
    tail_start(3)

    q_f = my_q.astype(jnp.float32)
    own_scores = [
        jnp.sum(q_f * new_kv[u:u + 1], axis=1, keepdims=True) * score_scale for u in range(STEPS)
    ]
    step_of = lax.shift_right_logical(lax.broadcasted_iota(jnp.int32, (QR, 1), 0), 3)
    own_scores = [jnp.where((step_of >= u) & (z == y), own_scores[u], NEG) for u in range(STEPS)]

    def merge(ref, count):
        tiles = [ref[i, pl.ds(QR, 8), :] for i in range(count)]
        ms = [jnp.concatenate([t[:, 0:1], t[:, 32:33]], axis=0) for t in tiles]
        ls = [jnp.concatenate([t[:, 64:65], t[:, 96:97]], axis=0) for t in tiles]
        return ms, ls, [ref[i, pl.ds(0, QR), :] for i in range(count)]

    def combine(ms, ls, os, m):
        factors = [jnp.exp(a - m) for a in ms]
        l = functools.reduce(lambda a, b: a + b, [f * a for f, a in zip(factors, ls)])
        o = functools.reduce(lambda a, b: a + b, [f * a for f, a in zip(factors, os)])
        return m, l, o

    wait()
    ms, ls, os = merge(rb1, ny)
    peak = functools.reduce(jnp.maximum, ms + own_scores)
    own = [jnp.exp(a - peak) for a in own_scores]
    _, l, o = combine(ms, ls, os, peak)
    for u, w in enumerate(own):
        l = l + w
        o = o + w.astype(jnp.bfloat16).astype(jnp.float32) * new_kv[STEPS + u:STEPS + u + 1]
    b2s[pl.ds(0, QR), :] = o
    b2s[pl.ds(QR, 8), :] = pack(peak, l)
    wait, copies = exchange(4, NZ, z_peer, z, lambda p: b2s, lambda m: rb2.at[m], zb_sem)
    sent += copies
    rb2[z] = b2s[...]
    tail_start(4)
    wait()
    ms, ls, os = merge(rb2, NZ)
    _, l, o = combine(ms, ls, os, functools.reduce(jnp.maximum, ms))
    att = (o / l).astype(jnp.bfloat16)
    asend[...] = att
    wait, copies = exchange(5, ny, y_peer, y, lambda p: asend, lambda m: abuf.at[q_rows(m)], yt_sem)
    sent += copies
    abuf[q_rows(y), :] = att
    tail_start(5)
    loads[8].wait()
    wait()
    attf[...] = abuf[...].astype(jnp.float32)
    att_all = jnp.concatenate([
        jnp.concatenate([attf[pl.ds(s * GROUP + g, ROWS, stride=QR), :] for s in range(STEPS)], axis=0)
        for g in range(GROUP)
    ], axis=1).astype(jnp.bfloat16)
    mine = nn(att_all, wo_v[...])
    csend[...] = mine
    wait, copies = exchange(6, nkv, kv_peer, kv, lambda p: csend, lambda m: rc.at[m], kv_sem)
    sent += copies
    rc[kv] = mine
    tail_start(6)
    wait()
    mixed[...] = functools.reduce(lambda a, b: a + b, [rc[i] for i in range(nkv)]).astype(jnp.bfloat16)

    for copy in sent:
        copy.wait_send()
    for kind in (2, 3):
        pltpu.make_async_copy(landing[kind], landing[kind], tail_recv.at[kind]).wait()
    for kind, ref in enumerate((stage_k, stage_v, got_k, got_v)):
        others = ref.at[pl.ds(0, len(tail_order[kind]))]
        pltpu.make_async_copy(others, others, tail_send.at[kind]).wait()


def store_body(nz, rows, got_k, got_v, mixed, out_k, out_v, bounds, sem):
    mixed[...] = rows[...]
    copies = [
        pltpu.make_async_copy(got, out, sem.at[i]) for i, (got, out) in enumerate(((got_k, out_k), (got_v, out_v)))
    ]
    for copy in copies:
        copy.start()
    count = got_k.shape[1] * PAIR

    def step(i, carry):
        pages = got_k[i].astype(jnp.float32).reshape(count, PAGE, HD)
        at = pl.ds(pl.multiple_of(i * count, count), count)
        bounds[at] = jnp.stack([jnp.min(pages, axis=1), jnp.max(pages, axis=1)], axis=1).astype(jnp.bfloat16)
        return carry

    lax.fori_loop(0, nz, step, 0)
    for copy in copies:
        copy.wait()


def on_device(
    hidden, w_qkv, w_out, key_pages, value_pages, ctx_len, selected,
    tail_keys, tail_values, tail_count, tail_dest,
):
    n_ctx = lax.axis_size("ctx")
    nkv = lax.axis_size("kv")
    ny = n_ctx // NZ
    pages_here = key_pages.shape[1]
    out_here = tail_keys.shape[0]
    tokens = pages_here * PAGE
    tail_tokens = out_here * PAGE
    bf, f32, i32 = jnp.bfloat16, jnp.float32, jnp.int32
    any_spec = pl.BlockSpec(memory_space=pltpu.HBM)
    smem = pl.BlockSpec(memory_space=pltpu.SMEM)
    vmem = pl.BlockSpec(memory_space=pltpu.VMEM)
    dma = pltpu.SemaphoreType.DMA
    tail_shape = (NZ, ny, PAIR, PAGE, HD)
    turned = (ny, NZ, PAIR, PAGE, HD)
    rows, got_k, got_v = pl.pallas_call(
        functools.partial(body, ny, nkv, out_here, pages_here),
        out_shape=(
            pltpu.VMEM((STEPS * ROWS, HD), bf),
            pltpu.VMEM(tail_shape, bf),
            pltpu.VMEM(tail_shape, bf),
        ),
        in_specs=[smem, smem] + [any_spec] * 9,
        out_specs=(vmem, vmem, vmem),
        scratch_shapes=[
            pltpu.VMEM((STEPS * ROWS, HD), bf),
            pltpu.VMEM(w_qkv.shape, bf),
            pltpu.VMEM(w_out.shape, bf),
            pltpu.VMEM((ROWS, tokens, HD), bf),
            pltpu.VMEM((ROWS, tokens, HD), bf),
            pltpu.VMEM(selected.shape, i32),
            pltpu.VMEM((1, 128), i32),
            pltpu.VMEM((out_here + 1, PAGE, HD), bf),
            pltpu.VMEM((out_here + 1, PAGE, HD), bf),
            pltpu.VMEM((ROWS * PIECE, HD), f32),
            pltpu.VMEM((NZ, PIECE, HD), f32),
            pltpu.VMEM((PIECE, HD), f32),
            pltpu.VMEM((ny, PIECE, HD), f32),
            pltpu.VMEM((QR, HD), bf),
            pltpu.VMEM((ROWS * QR, HD), bf),
            pltpu.VMEM((ROWS * STEPS, tokens), f32),
            pltpu.VMEM((ROWS * PIECE, HD), f32),
            pltpu.VMEM((ny, PIECE, HD), f32),
            pltpu.VMEM((PIECE, HD), f32),
            pltpu.VMEM((NZ, PIECE, HD), f32),
            pltpu.VMEM((QR, HD), bf),
            pltpu.VMEM((ROWS * QR, HD), bf),
            pltpu.VMEM((ROWS * QR, HD), f32),
            pltpu.VMEM((STEPS * ROWS, HD), f32),
            pltpu.VMEM((nkv, STEPS * ROWS, HD), f32),
            pltpu.VMEM(turned, bf),
            pltpu.VMEM(tail_shape, bf),
            pltpu.VMEM(turned, bf),
            pltpu.VMEM(tail_shape, bf),
            pltpu.VMEM((8, 128), i32),
            pltpu.SMEM((8, 128), i32),
            dma((9,)),
            dma((7, 8)),
            dma((NZ,)),
            dma((ny,)),
            dma((NZ,)),
            dma((ny,)),
            dma((NZ,)),
            dma((ny,)),
            dma((nkv,)),
            dma((4,)),
            dma((4,)),
            dma((1,)),
        ],
        compiler_params=pltpu.CompilerParams(
            collective_id=0, has_side_effects=True, vmem_limit_bytes=60 * 1024 * 1024
        ),
    )(
        ctx_len, tail_count, hidden.reshape(STEPS * ROWS, HD), w_qkv, w_out,
        key_pages.reshape(ROWS, tokens, HD), value_pages.reshape(ROWS, tokens, HD), selected,
        tail_keys, tail_values, tail_dest.T,
    )
    mixed, out_k, out_v, bounds = pl.pallas_call(
        functools.partial(store_body, NZ),
        out_shape=(
            jax.ShapeDtypeStruct((STEPS * ROWS, HD), bf),
            jax.ShapeDtypeStruct(tail_shape, bf),
            jax.ShapeDtypeStruct(tail_shape, bf),
            jax.ShapeDtypeStruct((n_ctx * PAIR, 2, HD), bf),
        ),
        in_specs=[vmem, vmem, vmem],
        out_specs=(vmem, any_spec, any_spec, vmem),
        scratch_shapes=[dma((2,))],
        compiler_params=pltpu.CompilerParams(vmem_limit_bytes=16 * 1024 * 1024),
    )(rows, got_k, got_v)
    return (
        mixed.reshape(STEPS, ROWS, HD),
        out_k.reshape(n_ctx * PAIR, PAGE, HD),
        out_v.reshape(n_ctx * PAIR, PAGE, HD),
        bounds,
    )


def solution(mesh):
    placed = (
        P(None, None, "ctx"),
        P("ctx", "kv"),
        P("kv", "ctx"),
        P(None, "ctx", None, "kv"),
        P(None, "ctx", None, "kv"),
        P(),
        P(None, None, "kv", None),
        P("ctx", None, "kv"),
        P("ctx", None, "kv"),
        P(),
        P(),
    )
    return jax.shard_map(
        on_device,
        mesh=mesh,
        in_specs=placed,
        out_specs=(
            P(None, None, "ctx"),
            P("ctx", None, "kv"),
            P("ctx", None, "kv"),
            P("ctx", None, "kv"),
        ),
        check_vma=False,
    )
```

```python
import functools
import math

import jax
import jax.numpy as jnp
from jax import lax
from jax.experimental import pallas as pl
from jax.experimental.pallas import tpu as pltpu
from jax.sharding import PartitionSpec as P

HD = 128
GROUP = 8
PAIR = 2
ROWS = 8
STEPS = 2
PAGE = 16
NZ = 8
QR = STEPS * GROUP
PIECE = 24
NEG = -1e30
MESH = pl.DeviceIdType.MESH
SCHEDULE = (((0, 3),), ((1, 3),), ((0, 4),), ((1, 4),), ((3, 3),), ((2, 3),), ((2, 4), (3, 4)), ())


def far_first(count):
    return sorted(range(1, count), key=lambda d: (-min(d, count - d), d))


def nt(a, b):
    return lax.dot_general(a, b, (((1,), (1,)), ((), ())), preferred_element_type=jnp.float32)


def nn(a, b):
    return jnp.dot(a, b, preferred_element_type=jnp.float32)


def body(
    ny, nkv, out_here, pages_here,
    ctx_len, tail_count, hidden, w_qkv, w_out, keys, values, selected, tail_k, tail_v, dest,
    mixed, got_k, got_v,
    hid_v, wq_v, wo_v, k_v, v_v, sel_v, dest_v, tk_v, tv_v,
    part, ra1, a2s, ra2, qsend, qbuf, bias, bsend, rb1, b2s, rb2, asend, abuf, attf, csend, rc,
    stage_k, stage_v, mid_k, mid_v, inv_v, inv_s,
    in_sem, send_sem, za_sem, ya_sem, zq_sem, yb_sem, zb_sem, yt_sem, kv_sem,
    tail_send, tail_recv, inv_sem,
):
    ctx = lax.axis_index("ctx")
    kv = lax.axis_index("kv")
    z = lax.div(ctx, ny)
    y = lax.rem(ctx, ny)
    n_ctx = NZ * ny
    score_scale = 1.0 / math.sqrt(HD)
    tokens = pages_here * PAGE
    tail_tokens = out_here * PAGE

    def z_peer(d):
        peer = lax.rem(z + d, NZ)
        return peer, (peer * ny + y, kv)

    def y_peer(d):
        peer = lax.rem(y + d, ny)
        return peer, (z * ny + peer, kv)

    def kv_peer(d):
        peer = lax.rem(kv + d, nkv)
        return peer, (ctx, peer)

    barrier = pltpu.get_barrier_semaphore()
    peers = NZ - 1 + ny - 1 + nkv - 1
    for count, peer_of in ((NZ, z_peer), (ny, y_peer), (nkv, kv_peer)):
        for d in far_first(count):
            pl.semaphore_signal(barrier, inc=1, device_id=peer_of(d)[1], device_id_type=MESH)

    first = lax.div(ctx * out_here, 128) * 128
    loads = [
        (hidden, hid_v),
        (w_qkv, wq_v),
        (dest.at[:, pl.ds(pl.multiple_of(first, 128), 128)], dest_v),
        (tail_k, tk_v.at[pl.ds(0, out_here)]),
        (tail_v, tv_v.at[pl.ds(0, out_here)]),
        (selected, sel_v),
        (keys, k_v),
        (values, v_v),
        (w_out, wo_v),
    ]
    loads = [pltpu.make_async_copy(a, b, in_sem.at[i]) for i, (a, b) in enumerate(loads)]
    for load in loads:
        load.start()

    loads[0].wait()
    loads[1].wait()
    proj = nn(hid_v[...], wq_v[...])
    for j in range(GROUP + 2):
        for s in range(STEPS):
            at = s * GROUP + j if j < GROUP else QR + (j - GROUP) * STEPS + s
            part[pl.ds(at, ROWS, stride=PIECE), :] = proj[s * ROWS:(s + 1) * ROWS, j * HD:(j + 1) * HD]

    tk_v[out_here] = jnp.zeros((PAGE, HD), jnp.bfloat16)
    tv_v[out_here] = jnp.zeros((PAGE, HD), jnp.bfloat16)
    loads[2].wait()
    offset = ctx * out_here - first
    sub = lax.broadcasted_iota(jnp.int32, (128, 128), 0)
    lane = lax.broadcasted_iota(jnp.int32, (128, 128), 1)
    lane_mine = (lane >= offset) & (lane < offset + out_here)
    sub_mine = (sub >= offset) & (sub < offset + out_here)
    dest_row = jnp.broadcast_to(dest_v[...], (128, 128))
    dest_col = jnp.sum(jnp.where(sub == lane, dest_row, 0), axis=1, keepdims=True)
    same = (dest_row == dest_col) & lane_mine & (lane < sub)
    rank_col = jnp.sum(jnp.where(same, 1, 0), axis=1, keepdims=True)
    target = dest_col * PAIR + rank_col
    hit = (lane == target) & sub_mine
    table = jnp.sum(jnp.where(hit, sub - offset - out_here, 0), axis=0, keepdims=True) + out_here
    inv_v[...] = jnp.broadcast_to(table, (8, 128))
    table_copy = pltpu.make_async_copy(inv_v, inv_s, inv_sem.at[0])
    table_copy.start()

    loads[3].wait()
    loads[4].wait()
    table_copy.wait()

    def place(d, carry):
        to_z = lax.div(d, ny)
        to_y = lax.rem(d, ny)
        for k in range(PAIR):
            page = inv_s[0, d * PAIR + k]
            stage_k[to_y, to_z, k] = tk_v[page]
            stage_v[to_z, to_y, k] = tv_v[page]
        return carry

    lax.fori_loop(0, n_ctx, place, 0)
    pl.semaphore_wait(barrier, peers)

    def piece(i):
        return pl.ds(pl.multiple_of(i * PIECE, 8), PIECE)

    def q_rows(i):
        return pl.ds(pl.multiple_of(i * QR, QR), QR)

    def exchange(phase, count, peer_of, me, src, dst, recv):
        copies = []
        for d in far_first(count):
            peer, device = peer_of(d)
            copy = pltpu.make_async_remote_copy(
                src_ref=src(peer), dst_ref=dst(me), send_sem=send_sem.at[phase, d], recv_sem=recv.at[me],
                device_id=device, device_id_type=MESH,
            )
            copy.start()
            copies.append(copy)

        def wait():
            for d in range(1, count):
                peer, device = peer_of(d)
                pltpu.make_async_remote_copy(
                    src_ref=src(peer), dst_ref=dst(peer), send_sem=send_sem.at[phase, d], recv_sem=recv.at[peer],
                    device_id=device, device_id_type=MESH,
                ).wait_recv()

        return wait, copies

    sent = []

    tail_peer = (y_peer, z_peer, z_peer, y_peer)
    tail_order = ((4, 2, 6, 3, 5, 1, 7), (4, 2, 6, 3, 5, 1, 7), (4, 2, 6, 3, 5, 1, 7), (4, 2, 6, 3, 5, 1, 7))
    tail_src = (
        lambda p: stage_k.at[p], lambda p: stage_v.at[p], lambda p: mid_k.at[:, p], lambda p: mid_v.at[:, p],
    )
    tail_dst = (mid_k.at[y], mid_v.at[z], got_k.at[z], got_v.at[:, y])
    tail_me = (y, z, z, y)
    landing = (mid_k, mid_v, got_k, got_v)
    begun = [0, 0, 0, 0]

    def tail_start(phase):
        for kind, number in SCHEDULE[phase]:
            if begun[kind] == 0:
                if kind >= 2:
                    pltpu.make_async_copy(landing[kind - 2], landing[kind - 2], tail_recv.at[kind - 2]).wait()
                pltpu.make_async_copy(tail_src[kind](tail_me[kind]), tail_dst[kind], tail_recv.at[kind]).start()
            for d in tail_order[kind][begun[kind]:begun[kind] + number]:
                peer, device = tail_peer[kind](d)
                pltpu.make_async_remote_copy(
                    src_ref=tail_src[kind](peer), dst_ref=tail_dst[kind], send_sem=tail_send.at[kind],
                    recv_sem=tail_recv.at[kind], device_id=device, device_id_type=MESH,
                ).start()
            begun[kind] += number

    wait, copies = exchange(0, NZ, z_peer, z, lambda p: part.at[piece(p)], lambda m: ra1.at[m], za_sem)
    sent += copies
    ra1[z] = part[piece(z), :]

    tail_start(0)

    wait()
    a2s[...] = functools.reduce(lambda a, b: a + b, [ra1[i] for i in range(NZ)])
    wait, copies = exchange(1, ny, y_peer, y, lambda p: a2s, lambda m: ra2.at[m], ya_sem)
    sent += copies
    ra2[y] = a2s[...]
    tail_start(1)

    loads[5].wait()
    token = lax.broadcasted_iota(jnp.int32, (1, tokens), 1)
    page = lax.shift_right_logical(token, 4)
    for r in range(ROWS):
        inside = ctx * tokens + token < ctx_len[r]
        for s in range(STEPS):
            rel = sel_v[s, r] - ctx * pages_here
            bit = lax.shift_left(jnp.ones_like(rel), jnp.bitwise_and(rel, 15)).astype(jnp.float32)
            low = jnp.sum(jnp.where((rel >= 0) & (rel < 16), bit, 0.0), axis=1, keepdims=True).astype(jnp.int32)
            high = jnp.sum(jnp.where((rel >= 16) & (rel < 32), bit, 0.0), axis=1, keepdims=True).astype(jnp.int32)
            word = jnp.where(page < 16, low, high)
            live = jnp.bitwise_and(lax.shift_right_logical(word, jnp.bitwise_and(page, 15)), 1) == 1
            bias[pl.ds(r * STEPS + s, 1), :] = jnp.where(live & inside, 0.0, NEG)

    wait()
    total = functools.reduce(lambda a, b: a + b, [ra2[i] for i in range(ny)])
    rounded = total.astype(jnp.bfloat16)
    my_q = rounded[:QR]
    new_kv = rounded.astype(jnp.float32)[QR:QR + 2 * STEPS]
    qsend[...] = my_q
    wait, copies = exchange(2, NZ, z_peer, z, lambda p: qsend, lambda m: qbuf.at[q_rows(m)], zq_sem)
    sent += copies
    qbuf[q_rows(z), :] = my_q
    tail_start(2)

    tail_token = lax.broadcasted_iota(jnp.int32, (1, tail_tokens), 1)
    slot = lax.shift_right_logical(tail_token, 4) + ctx * out_here
    tail_row = jnp.zeros((1, tail_tokens), jnp.int32)
    end = 0
    for r in range(ROWS):
        end = end + tail_count[r]
        tail_row = tail_row + jnp.where(slot >= end, 1, 0)
    loads[6].wait()
    loads[7].wait()
    wait()

    tail_start(7)
    q_all = qbuf[...]
    scores_t = nt(q_all, tk_v[pl.ds(0, out_here)].reshape(tail_tokens, HD)) * score_scale
    q_row = lax.shift_right_logical(lax.broadcasted_iota(jnp.int32, (ROWS * QR, tail_tokens), 0), 4)
    scores_t = jnp.where(q_row == tail_row, scores_t, NEG)
    peak_t = jnp.max(scores_t, axis=1, keepdims=True)
    scores_r, peaks = [], []
    for r in range(ROWS):
        masked = nt(q_all[r * QR:(r + 1) * QR], k_v[r]) * score_scale
        masked = jnp.concatenate([
            masked[s * GROUP:(s + 1) * GROUP] + bias[pl.ds(r * STEPS + s, 1), :] for s in range(STEPS)
        ], axis=0)
        scores_r.append(masked)
        peaks.append(jnp.maximum(jnp.max(masked, axis=1, keepdims=True), peak_t[r * QR:(r + 1) * QR]))
    weights_t = jnp.exp(scores_t - jnp.concatenate(peaks, axis=0))
    sums_t = jnp.sum(weights_t, axis=1, keepdims=True)
    out_t = nn(weights_t.astype(jnp.bfloat16), tv_v[pl.ds(0, out_here)].reshape(tail_tokens, HD))
    lanes = lax.broadcasted_iota(jnp.int32, (QR, HD), 1)

    def parts(v):
        high = v.astype(jnp.bfloat16).astype(jnp.float32)
        middle = (v - high).astype(jnp.bfloat16).astype(jnp.float32)
        return high, middle, v - high - middle

    def pack(m, l):
        tile = jnp.zeros((QR, HD), jnp.float32)
        for i, part_of in enumerate(parts(m) + parts(l)):
            tile = jnp.where(lanes == i, part_of, tile)
        return tile.astype(jnp.bfloat16)

    for r in range(ROWS):
        weights_r = jnp.exp(scores_r[r] - peaks[r])
        sums = jnp.sum(weights_r, axis=1, keepdims=True) + sums_t[r * QR:(r + 1) * QR]
        out_r = nn(weights_r.astype(jnp.bfloat16), v_v[r]) + out_t[r * QR:(r + 1) * QR]
        bsend[r, pl.ds(0, QR), :] = out_r.astype(jnp.bfloat16)
        bsend[r, pl.ds(QR, QR), :] = pack(peaks[r], sums)

    wait, copies = exchange(3, ny, y_peer, y, lambda p: bsend.at[p], lambda m: rb1.at[m], yb_sem)
    sent += copies
    rb1[y] = bsend[y]
    tail_start(3)

    q_f = my_q.astype(jnp.float32)
    own_scores = [
        jnp.sum(q_f * new_kv[u:u + 1], axis=1, keepdims=True) * score_scale for u in range(STEPS)
    ]
    step_of = lax.shift_right_logical(lax.broadcasted_iota(jnp.int32, (QR, 1), 0), 3)
    own_scores = [jnp.where((step_of >= u) & (z == y), own_scores[u], NEG) for u in range(STEPS)]

    def merge(ref, count):
        tiles = [ref[i, pl.ds(QR, QR), :].astype(jnp.float32) for i in range(count)]
        ms = [t[:, 0:1] + t[:, 1:2] + t[:, 2:3] for t in tiles]
        ls = [t[:, 3:4] + t[:, 4:5] + t[:, 5:6] for t in tiles]
        return ms, ls, [ref[i, pl.ds(0, QR), :].astype(jnp.float32) for i in range(count)]

    def combine(ms, ls, os, m):
        factors = [jnp.exp(a - m) for a in ms]
        l = functools.reduce(lambda a, b: a + b, [f * a for f, a in zip(factors, ls)])
        o = functools.reduce(lambda a, b: a + b, [f * a for f, a in zip(factors, os)])
        return m, l, o

    wait()
    ms, ls, os = merge(rb1, ny)
    peak = functools.reduce(jnp.maximum, ms + own_scores)
    own = [jnp.exp(a - peak) for a in own_scores]
    _, l, o = combine(ms, ls, os, peak)
    for u, w in enumerate(own):
        l = l + w
        o = o + w.astype(jnp.bfloat16).astype(jnp.float32) * new_kv[STEPS + u:STEPS + u + 1]
    b2s[pl.ds(0, QR), :] = o.astype(jnp.bfloat16)
    b2s[pl.ds(QR, QR), :] = pack(peak, l)
    wait, copies = exchange(4, NZ, z_peer, z, lambda p: b2s, lambda m: rb2.at[m], zb_sem)
    sent += copies
    rb2[z] = b2s[...]
    tail_start(4)
    wait()
    ms, ls, os = merge(rb2, NZ)
    _, l, o = combine(ms, ls, os, functools.reduce(jnp.maximum, ms))
    att = (o / l).astype(jnp.bfloat16)
    asend[...] = att
    wait, copies = exchange(5, ny, y_peer, y, lambda p: asend, lambda m: abuf.at[q_rows(m)], yt_sem)
    sent += copies
    abuf[q_rows(y), :] = att
    tail_start(5)
    loads[8].wait()
    wait()
    attf[...] = abuf[...].astype(jnp.float32)
    att_all = jnp.concatenate([
        jnp.concatenate([attf[pl.ds(s * GROUP + g, ROWS, stride=QR), :] for s in range(STEPS)], axis=0)
        for g in range(GROUP)
    ], axis=1).astype(jnp.bfloat16)
    mine = nn(att_all, wo_v[...])
    csend[...] = mine
    wait, copies = exchange(6, nkv, kv_peer, kv, lambda p: csend, lambda m: rc.at[m], kv_sem)
    sent += copies
    rc[kv] = mine
    tail_start(6)
    wait()
    mixed[...] = functools.reduce(lambda a, b: a + b, [rc[i] for i in range(nkv)]).astype(jnp.bfloat16)

    for copy in sent:
        copy.wait_send()
    for kind in (2, 3):
        pltpu.make_async_copy(landing[kind], landing[kind], tail_recv.at[kind]).wait()
    for kind, ref in enumerate((stage_k, stage_v, got_k, got_v)):
        others = ref.at[pl.ds(0, len(tail_order[kind]))]
        pltpu.make_async_copy(others, others, tail_send.at[kind]).wait()


def store_body(nz, rows, got_k, got_v, mixed, out_k, out_v, bounds, sem):
    mixed[...] = rows[...]
    copies = [
        pltpu.make_async_copy(got, out, sem.at[i]) for i, (got, out) in enumerate(((got_k, out_k), (got_v, out_v)))
    ]
    for copy in copies:
        copy.start()
    count = got_k.shape[1] * PAIR

    def step(i, carry):
        pages = got_k[i].astype(jnp.float32).reshape(count, PAGE, HD)
        at = pl.ds(pl.multiple_of(i * count, count), count)
        bounds[at] = jnp.stack([jnp.min(pages, axis=1), jnp.max(pages, axis=1)], axis=1).astype(jnp.bfloat16)
        return carry

    lax.fori_loop(0, nz, step, 0)
    for copy in copies:
        copy.wait()


def on_device(
    hidden, w_qkv, w_out, key_pages, value_pages, ctx_len, selected,
    tail_keys, tail_values, tail_count, tail_dest,
):
    n_ctx = lax.axis_size("ctx")
    nkv = lax.axis_size("kv")
    ny = n_ctx // NZ
    pages_here = key_pages.shape[1]
    out_here = tail_keys.shape[0]
    tokens = pages_here * PAGE
    tail_tokens = out_here * PAGE
    bf, f32, i32 = jnp.bfloat16, jnp.float32, jnp.int32
    any_spec = pl.BlockSpec(memory_space=pltpu.HBM)
    smem = pl.BlockSpec(memory_space=pltpu.SMEM)
    vmem = pl.BlockSpec(memory_space=pltpu.VMEM)
    dma = pltpu.SemaphoreType.DMA
    tail_shape = (NZ, ny, PAIR, PAGE, HD)
    turned = (ny, NZ, PAIR, PAGE, HD)
    rows, got_k, got_v = pl.pallas_call(
        functools.partial(body, ny, nkv, out_here, pages_here),
        out_shape=(
            pltpu.VMEM((STEPS * ROWS, HD), bf),
            pltpu.VMEM(tail_shape, bf),
            pltpu.VMEM(tail_shape, bf),
        ),
        in_specs=[smem, smem] + [any_spec] * 9,
        out_specs=(vmem, vmem, vmem),
        scratch_shapes=[
            pltpu.VMEM((STEPS * ROWS, HD), bf),
            pltpu.VMEM(w_qkv.shape, bf),
            pltpu.VMEM(w_out.shape, bf),
            pltpu.VMEM((ROWS, tokens, HD), bf),
            pltpu.VMEM((ROWS, tokens, HD), bf),
            pltpu.VMEM(selected.shape, i32),
            pltpu.VMEM((1, 128), i32),
            pltpu.VMEM((out_here + 1, PAGE, HD), bf),
            pltpu.VMEM((out_here + 1, PAGE, HD), bf),
            pltpu.VMEM((ROWS * PIECE, HD), f32),
            pltpu.VMEM((NZ, PIECE, HD), f32),
            pltpu.VMEM((PIECE, HD), f32),
            pltpu.VMEM((ny, PIECE, HD), f32),
            pltpu.VMEM((QR, HD), bf),
            pltpu.VMEM((ROWS * QR, HD), bf),
            pltpu.VMEM((ROWS * STEPS, tokens), f32),
            pltpu.VMEM((ROWS, 2 * QR, HD), bf),
            pltpu.VMEM((ny, 2 * QR, HD), bf),
            pltpu.VMEM((2 * QR, HD), bf),
            pltpu.VMEM((NZ, 2 * QR, HD), bf),
            pltpu.VMEM((QR, HD), bf),
            pltpu.VMEM((ROWS * QR, HD), bf),
            pltpu.VMEM((ROWS * QR, HD), f32),
            pltpu.VMEM((STEPS * ROWS, HD), f32),
            pltpu.VMEM((nkv, STEPS * ROWS, HD), f32),
            pltpu.VMEM(turned, bf),
            pltpu.VMEM(tail_shape, bf),
            pltpu.VMEM(turned, bf),
            pltpu.VMEM(tail_shape, bf),
            pltpu.VMEM((8, 128), i32),
            pltpu.SMEM((8, 128), i32),
            dma((9,)),
            dma((7, 8)),
            dma((NZ,)),
            dma((ny,)),
            dma((NZ,)),
            dma((ny,)),
            dma((NZ,)),
            dma((ny,)),
            dma((nkv,)),
            dma((4,)),
            dma((4,)),
            dma((1,)),
        ],
        compiler_params=pltpu.CompilerParams(
            collective_id=0, has_side_effects=True, vmem_limit_bytes=60 * 1024 * 1024
        ),
    )(
        ctx_len, tail_count, hidden.reshape(STEPS * ROWS, HD), w_qkv, w_out,
        key_pages.reshape(ROWS, tokens, HD), value_pages.reshape(ROWS, tokens, HD), selected,
        tail_keys, tail_values, tail_dest.T,
    )
    mixed, out_k, out_v, bounds = pl.pallas_call(
        functools.partial(store_body, NZ),
        out_shape=(
            jax.ShapeDtypeStruct((STEPS * ROWS, HD), bf),
            jax.ShapeDtypeStruct(tail_shape, bf),
            jax.ShapeDtypeStruct(tail_shape, bf),
            jax.ShapeDtypeStruct((n_ctx * PAIR, 2, HD), bf),
        ),
        in_specs=[vmem, vmem, vmem],
        out_specs=(vmem, any_spec, any_spec, vmem),
        scratch_shapes=[dma((2,))],
        compiler_params=pltpu.CompilerParams(vmem_limit_bytes=16 * 1024 * 1024),
    )(rows, got_k, got_v)
    return (
        mixed.reshape(STEPS, ROWS, HD),
        out_k.reshape(n_ctx * PAIR, PAGE, HD),
        out_v.reshape(n_ctx * PAIR, PAGE, HD),
        bounds,
    )


def solution(mesh):
    placed = (
        P(None, None, "ctx"),
        P("ctx", "kv"),
        P("kv", "ctx"),
        P(None, "ctx", None, "kv"),
        P(None, "ctx", None, "kv"),
        P(),
        P(None, None, "kv", None),
        P("ctx", None, "kv"),
        P("ctx", None, "kv"),
        P(),
        P(),
    )
    return jax.shard_map(
        on_device,
        mesh=mesh,
        in_specs=placed,
        out_specs=(
            P(None, None, "ctx"),
            P("ctx", None, "kv"),
            P("ctx", None, "kv"),
            P("ctx", None, "kv"),
        ),
        check_vma=False,
    )
```

```python
import functools
import math

import jax
import jax.numpy as jnp
from jax import lax
from jax.experimental import pallas as pl
from jax.experimental.pallas import tpu as pltpu
from jax.sharding import PartitionSpec as P

HD = 128
GROUP = 8
PAIR = 2
ROWS = 8
STEPS = 2
PAGE = 16
NZ = 8
QR = STEPS * GROUP
PIECE = 24
NEG = -1e30
MESH = pl.DeviceIdType.MESH
SCHEDULE = (((0, 3),), ((1, 3),), ((0, 4),), ((1, 4),), ((3, 3),), ((2, 3),), ((3, 1), (2, 1), (3, 1), (2, 1), (3, 1), (2, 1), (3, 1), (2, 1)), ())


TAIL_ORDER = (4, 1, 7, 3, 5, 2, 6)


def far_first(count):
    return sorted(range(1, count), key=lambda d: (-min(d, count - d), d))


def nt(a, b):
    return lax.dot_general(a, b, (((1,), (1,)), ((), ())), preferred_element_type=jnp.float32)


def nn(a, b):
    return jnp.dot(a, b, preferred_element_type=jnp.float32)


def body(
    ny, nkv, out_here, pages_here,
    ctx_len, tail_count, hidden, w_qkv, w_out, keys, values, selected, tail_k, tail_v, dest,
    mixed, got_k, got_v,
    hid_v, wq_v, wo_v, k_v, v_v, sel_v, dest_v, tk_v, tv_v,
    part, ra1, a2s, ra2, qsend, qbuf, bias, bsend, rb1, b2s, rb2, asend, abuf, attf, csend, rc,
    stage_k, stage_v, mid_k, mid_v, inv_v, inv_s,
    in_sem, send_sem, za_sem, ya_sem, zq_sem, yb_sem, zb_sem, yt_sem, kv_sem,
    tail_send, tail_recv, inv_sem,
):
    ctx = lax.axis_index("ctx")
    kv = lax.axis_index("kv")
    z = lax.div(ctx, ny)
    y = lax.rem(ctx, ny)
    n_ctx = NZ * ny
    score_scale = 1.0 / math.sqrt(HD)
    tokens = pages_here * PAGE
    tail_tokens = out_here * PAGE

    def z_peer(d):
        peer = lax.rem(z + d, NZ)
        return peer, (peer * ny + y, kv)

    def y_peer(d):
        peer = lax.rem(y + d, ny)
        return peer, (z * ny + peer, kv)

    def kv_peer(d):
        peer = lax.rem(kv + d, nkv)
        return peer, (ctx, peer)

    barrier = pltpu.get_barrier_semaphore()
    peers = NZ - 1 + ny - 1 + nkv - 1
    for count, peer_of in ((NZ, z_peer), (ny, y_peer), (nkv, kv_peer)):
        for d in far_first(count):
            pl.semaphore_signal(barrier, inc=1, device_id=peer_of(d)[1], device_id_type=MESH)

    first = lax.div(ctx * out_here, 128) * 128
    loads = [
        (hidden, hid_v),
        (w_qkv, wq_v),
        (dest.at[:, pl.ds(pl.multiple_of(first, 128), 128)], dest_v),
        (tail_k, tk_v.at[pl.ds(0, out_here)]),
        (tail_v, tv_v.at[pl.ds(0, out_here)]),
        (selected, sel_v),
        (keys, k_v),
        (values, v_v),
        (w_out, wo_v),
    ]
    loads = [pltpu.make_async_copy(a, b, in_sem.at[i]) for i, (a, b) in enumerate(loads)]
    for load in loads:
        load.start()

    loads[0].wait()
    loads[1].wait()
    proj = nn(hid_v[...], wq_v[...])
    for j in range(GROUP + 2):
        for s in range(STEPS):
            at = s * GROUP + j if j < GROUP else QR + (j - GROUP) * STEPS + s
            part[pl.ds(at, ROWS, stride=PIECE), :] = proj[s * ROWS:(s + 1) * ROWS, j * HD:(j + 1) * HD]

    tk_v[out_here] = jnp.zeros((PAGE, HD), jnp.bfloat16)
    tv_v[out_here] = jnp.zeros((PAGE, HD), jnp.bfloat16)
    loads[2].wait()
    offset = ctx * out_here - first
    sub = lax.broadcasted_iota(jnp.int32, (128, 128), 0)
    lane = lax.broadcasted_iota(jnp.int32, (128, 128), 1)
    lane_mine = (lane >= offset) & (lane < offset + out_here)
    sub_mine = (sub >= offset) & (sub < offset + out_here)
    dest_row = jnp.broadcast_to(dest_v[...], (128, 128))
    dest_col = jnp.sum(jnp.where(sub == lane, dest_row, 0), axis=1, keepdims=True)
    same = (dest_row == dest_col) & lane_mine & (lane < sub)
    rank_col = jnp.sum(jnp.where(same, 1, 0), axis=1, keepdims=True)
    target = dest_col * PAIR + rank_col
    hit = (lane == target) & sub_mine
    table = jnp.sum(jnp.where(hit, sub - offset - out_here, 0), axis=0, keepdims=True) + out_here
    inv_v[...] = jnp.broadcast_to(table, (8, 128))
    table_copy = pltpu.make_async_copy(inv_v, inv_s, inv_sem.at[0])
    table_copy.start()

    loads[3].wait()
    loads[4].wait()
    table_copy.wait()

    def place(d, carry):
        to_z = lax.div(d, ny)
        to_y = lax.rem(d, ny)
        for k in range(PAIR):
            page = inv_s[0, d * PAIR + k]
            stage_k[to_y, to_z, k] = tk_v[page]
            stage_v[to_z, to_y, k] = tv_v[page]
        return carry

    lax.fori_loop(0, n_ctx, place, 0)
    pl.semaphore_wait(barrier, peers)

    def piece(i):
        return pl.ds(pl.multiple_of(i * PIECE, 8), PIECE)

    def q_rows(i):
        return pl.ds(pl.multiple_of(i * QR, QR), QR)

    def exchange(phase, count, peer_of, me, src, dst, recv):
        copies = []
        for d in far_first(count):
            peer, device = peer_of(d)
            copy = pltpu.make_async_remote_copy(
                src_ref=src(peer), dst_ref=dst(me), send_sem=send_sem.at[phase, d], recv_sem=recv.at[me],
                device_id=device, device_id_type=MESH,
            )
            copy.start()
            copies.append(copy)

        def wait():
            for d in range(1, count):
                peer, device = peer_of(d)
                pltpu.make_async_remote_copy(
                    src_ref=src(peer), dst_ref=dst(peer), send_sem=send_sem.at[phase, d], recv_sem=recv.at[peer],
                    device_id=device, device_id_type=MESH,
                ).wait_recv()

        return wait, copies

    sent = []

    tail_peer = (y_peer, z_peer, z_peer, y_peer)
    tail_order = (TAIL_ORDER,) * 4
    tail_src = (
        lambda p: stage_k.at[p], lambda p: stage_v.at[p], lambda p: mid_k.at[:, p], lambda p: mid_v.at[:, p],
    )
    tail_dst = (mid_k.at[y], mid_v.at[z], got_k.at[z], got_v.at[:, y])
    tail_me = (y, z, z, y)
    landing = (mid_k, mid_v, got_k, got_v)
    begun = [0, 0, 0, 0]

    def tail_start(phase):
        for kind, number in SCHEDULE[phase]:
            if begun[kind] == 0:
                if kind >= 2:
                    pltpu.make_async_copy(landing[kind - 2], landing[kind - 2], tail_recv.at[kind - 2]).wait()
                pltpu.make_async_copy(tail_src[kind](tail_me[kind]), tail_dst[kind], tail_recv.at[kind]).start()
            for d in tail_order[kind][begun[kind]:begun[kind] + number]:
                peer, device = tail_peer[kind](d)
                pltpu.make_async_remote_copy(
                    src_ref=tail_src[kind](peer), dst_ref=tail_dst[kind], send_sem=tail_send.at[kind],
                    recv_sem=tail_recv.at[kind], device_id=device, device_id_type=MESH,
                ).start()
            begun[kind] += number

    wait, copies = exchange(0, NZ, z_peer, z, lambda p: part.at[piece(p)], lambda m: ra1.at[m], za_sem)
    sent += copies
    ra1[z] = part[piece(z), :]

    tail_start(0)

    wait()
    a2s[...] = functools.reduce(lambda a, b: a + b, [ra1[i] for i in range(NZ)])
    wait, copies = exchange(1, ny, y_peer, y, lambda p: a2s, lambda m: ra2.at[m], ya_sem)
    sent += copies
    ra2[y] = a2s[...]
    tail_start(1)

    loads[5].wait()
    token = lax.broadcasted_iota(jnp.int32, (1, tokens), 1)
    page = lax.shift_right_logical(token, 4)
    for r in range(ROWS):
        inside = ctx * tokens + token < ctx_len[r]
        for s in range(STEPS):
            rel = sel_v[s, r] - ctx * pages_here
            bit = lax.shift_left(jnp.ones_like(rel), jnp.bitwise_and(rel, 15)).astype(jnp.float32)
            low = jnp.sum(jnp.where((rel >= 0) & (rel < 16), bit, 0.0), axis=1, keepdims=True).astype(jnp.int32)
            high = jnp.sum(jnp.where((rel >= 16) & (rel < 32), bit, 0.0), axis=1, keepdims=True).astype(jnp.int32)
            word = jnp.where(page < 16, low, high)
            live = jnp.bitwise_and(lax.shift_right_logical(word, jnp.bitwise_and(page, 15)), 1) == 1
            bias[pl.ds(r * STEPS + s, 1), :] = jnp.where(live & inside, 0.0, NEG)

    wait()
    total = functools.reduce(lambda a, b: a + b, [ra2[i] for i in range(ny)])
    rounded = total.astype(jnp.bfloat16)
    my_q = rounded[:QR]
    new_kv = rounded.astype(jnp.float32)[QR:QR + 2 * STEPS]
    qsend[...] = my_q
    wait, copies = exchange(2, NZ, z_peer, z, lambda p: qsend, lambda m: qbuf.at[q_rows(m)], zq_sem)
    sent += copies
    qbuf[q_rows(z), :] = my_q
    tail_start(2)

    tail_token = lax.broadcasted_iota(jnp.int32, (1, tail_tokens), 1)
    slot = lax.shift_right_logical(tail_token, 4) + ctx * out_here
    tail_row = jnp.zeros((1, tail_tokens), jnp.int32)
    end = 0
    for r in range(ROWS):
        end = end + tail_count[r]
        tail_row = tail_row + jnp.where(slot >= end, 1, 0)
    loads[6].wait()
    loads[7].wait()
    wait()

    tail_start(7)
    q_all = qbuf[...]
    scores_t = nt(q_all, tk_v[pl.ds(0, out_here)].reshape(tail_tokens, HD)) * score_scale
    q_row = lax.shift_right_logical(lax.broadcasted_iota(jnp.int32, (ROWS * QR, tail_tokens), 0), 4)
    scores_t = jnp.where(q_row == tail_row, scores_t, NEG)
    peak_t = jnp.max(scores_t, axis=1, keepdims=True)
    scores_r, peaks = [], []
    for r in range(ROWS):
        masked = nt(q_all[r * QR:(r + 1) * QR], k_v[r]) * score_scale
        masked = jnp.concatenate([
            masked[s * GROUP:(s + 1) * GROUP] + bias[pl.ds(r * STEPS + s, 1), :] for s in range(STEPS)
        ], axis=0)
        scores_r.append(masked)
        peaks.append(jnp.maximum(jnp.max(masked, axis=1, keepdims=True), peak_t[r * QR:(r + 1) * QR]))
    weights_t = jnp.exp(scores_t - jnp.concatenate(peaks, axis=0))
    sums_t = jnp.sum(weights_t, axis=1, keepdims=True)
    out_t = nn(weights_t.astype(jnp.bfloat16), tv_v[pl.ds(0, out_here)].reshape(tail_tokens, HD))
    lanes = lax.broadcasted_iota(jnp.int32, (QR, HD), 1)

    def parts(v):
        high = v.astype(jnp.bfloat16).astype(jnp.float32)
        middle = (v - high).astype(jnp.bfloat16).astype(jnp.float32)
        return high, middle, v - high - middle

    def pack(m, l):
        tile = jnp.zeros((QR, HD), jnp.float32)
        for i, part_of in enumerate(parts(m) + parts(l)):
            tile = jnp.where(lanes == i, part_of, tile)
        return tile.astype(jnp.bfloat16)

    for r in range(ROWS):
        weights_r = jnp.exp(scores_r[r] - peaks[r])
        sums = jnp.sum(weights_r, axis=1, keepdims=True) + sums_t[r * QR:(r + 1) * QR]
        out_r = nn(weights_r.astype(jnp.bfloat16), v_v[r]) + out_t[r * QR:(r + 1) * QR]
        bsend[r, pl.ds(0, QR), :] = out_r.astype(jnp.bfloat16)
        bsend[r, pl.ds(QR, QR), :] = pack(peaks[r], sums)

    wait, copies = exchange(3, ny, y_peer, y, lambda p: bsend.at[p], lambda m: rb1.at[m], yb_sem)
    sent += copies
    rb1[y] = bsend[y]
    tail_start(3)

    q_f = my_q.astype(jnp.float32)
    own_scores = [
        jnp.sum(q_f * new_kv[u:u + 1], axis=1, keepdims=True) * score_scale for u in range(STEPS)
    ]
    step_of = lax.shift_right_logical(lax.broadcasted_iota(jnp.int32, (QR, 1), 0), 3)
    own_scores = [jnp.where((step_of >= u) & (z == y), own_scores[u], NEG) for u in range(STEPS)]

    def merge(ref, count):
        tiles = [ref[i, pl.ds(QR, QR), :].astype(jnp.float32) for i in range(count)]
        ms = [t[:, 0:1] + t[:, 1:2] + t[:, 2:3] for t in tiles]
        ls = [t[:, 3:4] + t[:, 4:5] + t[:, 5:6] for t in tiles]
        return ms, ls, [ref[i, pl.ds(0, QR), :].astype(jnp.float32) for i in range(count)]

    def combine(ms, ls, os, m):
        factors = [jnp.exp(a - m) for a in ms]
        l = functools.reduce(lambda a, b: a + b, [f * a for f, a in zip(factors, ls)])
        o = functools.reduce(lambda a, b: a + b, [f * a for f, a in zip(factors, os)])
        return m, l, o

    wait()
    ms, ls, os = merge(rb1, ny)
    peak = functools.reduce(jnp.maximum, ms + own_scores)
    own = [jnp.exp(a - peak) for a in own_scores]
    _, l, o = combine(ms, ls, os, peak)
    for u, w in enumerate(own):
        l = l + w
        o = o + w.astype(jnp.bfloat16).astype(jnp.float32) * new_kv[STEPS + u:STEPS + u + 1]
    b2s[pl.ds(0, QR), :] = o.astype(jnp.bfloat16)
    b2s[pl.ds(QR, QR), :] = pack(peak, l)
    wait, copies = exchange(4, NZ, z_peer, z, lambda p: b2s, lambda m: rb2.at[m], zb_sem)
    sent += copies
    rb2[z] = b2s[...]
    tail_start(4)
    wait()
    ms, ls, os = merge(rb2, NZ)
    _, l, o = combine(ms, ls, os, functools.reduce(jnp.maximum, ms))
    att = (o / l).astype(jnp.bfloat16)
    asend[...] = att
    wait, copies = exchange(5, ny, y_peer, y, lambda p: asend, lambda m: abuf.at[q_rows(m)], yt_sem)
    sent += copies
    abuf[q_rows(y), :] = att
    tail_start(5)
    loads[8].wait()
    wait()
    attf[...] = abuf[...].astype(jnp.float32)
    att_all = jnp.concatenate([
        jnp.concatenate([attf[pl.ds(s * GROUP + g, ROWS, stride=QR), :] for s in range(STEPS)], axis=0)
        for g in range(GROUP)
    ], axis=1).astype(jnp.bfloat16)
    mine = nn(att_all, wo_v[...])
    csend[...] = mine
    wait, copies = exchange(6, nkv, kv_peer, kv, lambda p: csend, lambda m: rc.at[m], kv_sem)
    sent += copies
    rc[kv] = mine
    tail_start(6)
    for copy in sent[:-len(copies)]:
        copy.wait_send()
    wait()
    mixed[...] = functools.reduce(lambda a, b: a + b, [rc[i] for i in range(nkv)]).astype(jnp.bfloat16)

    for copy in copies:
        copy.wait_send()
    for kind in (2, 3):
        pltpu.make_async_copy(landing[kind], landing[kind], tail_recv.at[kind]).wait()
    for kind, ref in enumerate((stage_k, stage_v, got_k, got_v)):
        others = ref.at[pl.ds(0, len(tail_order[kind]))]
        pltpu.make_async_copy(others, others, tail_send.at[kind]).wait()


def store_body(nz, rows, got_k, got_v, mixed, out_k, out_v, bounds, sem):
    mixed[...] = rows[...]
    copies = [
        pltpu.make_async_copy(got, out, sem.at[i]) for i, (got, out) in enumerate(((got_k, out_k), (got_v, out_v)))
    ]
    for copy in copies:
        copy.start()
    count = got_k.shape[1] * PAIR

    def step(i, carry):
        pages = got_k[i].astype(jnp.float32).reshape(count, PAGE, HD)
        at = pl.ds(pl.multiple_of(i * count, count), count)
        bounds[at] = jnp.stack([jnp.min(pages, axis=1), jnp.max(pages, axis=1)], axis=1).astype(jnp.bfloat16)
        return carry

    lax.fori_loop(0, nz, step, 0)
    for copy in copies:
        copy.wait()


def on_device(
    hidden, w_qkv, w_out, key_pages, value_pages, ctx_len, selected,
    tail_keys, tail_values, tail_count, tail_dest,
):
    n_ctx = lax.axis_size("ctx")
    nkv = lax.axis_size("kv")
    ny = n_ctx // NZ
    pages_here = key_pages.shape[1]
    out_here = tail_keys.shape[0]
    tokens = pages_here * PAGE
    tail_tokens = out_here * PAGE
    bf, f32, i32 = jnp.bfloat16, jnp.float32, jnp.int32
    any_spec = pl.BlockSpec(memory_space=pltpu.HBM)
    smem = pl.BlockSpec(memory_space=pltpu.SMEM)
    vmem = pl.BlockSpec(memory_space=pltpu.VMEM)
    dma = pltpu.SemaphoreType.DMA
    tail_shape = (NZ, ny, PAIR, PAGE, HD)
    turned = (ny, NZ, PAIR, PAGE, HD)
    rows, got_k, got_v = pl.pallas_call(
        functools.partial(body, ny, nkv, out_here, pages_here),
        out_shape=(
            pltpu.VMEM((STEPS * ROWS, HD), bf),
            pltpu.VMEM(tail_shape, bf),
            pltpu.VMEM(tail_shape, bf),
        ),
        in_specs=[smem, smem] + [any_spec] * 9,
        out_specs=(vmem, vmem, vmem),
        scratch_shapes=[
            pltpu.VMEM((STEPS * ROWS, HD), bf),
            pltpu.VMEM(w_qkv.shape, bf),
            pltpu.VMEM(w_out.shape, bf),
            pltpu.VMEM((ROWS, tokens, HD), bf),
            pltpu.VMEM((ROWS, tokens, HD), bf),
            pltpu.VMEM(selected.shape, i32),
            pltpu.VMEM((1, 128), i32),
            pltpu.VMEM((out_here + 1, PAGE, HD), bf),
            pltpu.VMEM((out_here + 1, PAGE, HD), bf),
            pltpu.VMEM((ROWS * PIECE, HD), f32),
            pltpu.VMEM((NZ, PIECE, HD), f32),
            pltpu.VMEM((PIECE, HD), f32),
            pltpu.VMEM((ny, PIECE, HD), f32),
            pltpu.VMEM((QR, HD), bf),
            pltpu.VMEM((ROWS * QR, HD), bf),
            pltpu.VMEM((ROWS * STEPS, tokens), f32),
            pltpu.VMEM((ROWS, 2 * QR, HD), bf),
            pltpu.VMEM((ny, 2 * QR, HD), bf),
            pltpu.VMEM((2 * QR, HD), bf),
            pltpu.VMEM((NZ, 2 * QR, HD), bf),
            pltpu.VMEM((QR, HD), bf),
            pltpu.VMEM((ROWS * QR, HD), bf),
            pltpu.VMEM((ROWS * QR, HD), f32),
            pltpu.VMEM((STEPS * ROWS, HD), f32),
            pltpu.VMEM((nkv, STEPS * ROWS, HD), f32),
            pltpu.VMEM(turned, bf),
            pltpu.VMEM(tail_shape, bf),
            pltpu.VMEM(turned, bf),
            pltpu.VMEM(tail_shape, bf),
            pltpu.VMEM((8, 128), i32),
            pltpu.SMEM((8, 128), i32),
            dma((9,)),
            dma((7, 8)),
            dma((NZ,)),
            dma((ny,)),
            dma((NZ,)),
            dma((ny,)),
            dma((NZ,)),
            dma((ny,)),
            dma((nkv,)),
            dma((4,)),
            dma((4,)),
            dma((1,)),
        ],
        compiler_params=pltpu.CompilerParams(
            collective_id=0, has_side_effects=True, vmem_limit_bytes=60 * 1024 * 1024
        ),
    )(
        ctx_len, tail_count, hidden.reshape(STEPS * ROWS, HD), w_qkv, w_out,
        key_pages.reshape(ROWS, tokens, HD), value_pages.reshape(ROWS, tokens, HD), selected,
        tail_keys, tail_values, tail_dest.T,
    )
    mixed, out_k, out_v, bounds = pl.pallas_call(
        functools.partial(store_body, NZ),
        out_shape=(
            jax.ShapeDtypeStruct((STEPS * ROWS, HD), bf),
            jax.ShapeDtypeStruct(tail_shape, bf),
            jax.ShapeDtypeStruct(tail_shape, bf),
            jax.ShapeDtypeStruct((n_ctx * PAIR, 2, HD), bf),
        ),
        in_specs=[vmem, vmem, vmem],
        out_specs=(vmem, any_spec, any_spec, vmem),
        scratch_shapes=[dma((2,))],
        compiler_params=pltpu.CompilerParams(vmem_limit_bytes=16 * 1024 * 1024),
    )(rows, got_k, got_v)
    return (
        mixed.reshape(STEPS, ROWS, HD),
        out_k.reshape(n_ctx * PAIR, PAGE, HD),
        out_v.reshape(n_ctx * PAIR, PAGE, HD),
        bounds,
    )


def solution(mesh):
    placed = (
        P(None, None, "ctx"),
        P("ctx", "kv"),
        P("kv", "ctx"),
        P(None, "ctx", None, "kv"),
        P(None, "ctx", None, "kv"),
        P(),
        P(None, None, "kv", None),
        P("ctx", None, "kv"),
        P("ctx", None, "kv"),
        P(),
        P(),
    )
    return jax.shard_map(
        on_device,
        mesh=mesh,
        in_specs=placed,
        out_specs=(
            P(None, None, "ctx"),
            P("ctx", None, "kv"),
            P("ctx", None, "kv"),
            P("ctx", None, "kv"),
        ),
        check_vma=False,
    )
```

```python
import functools
import math

import jax
import jax.numpy as jnp
from jax import lax
from jax.experimental import pallas as pl
from jax.experimental.pallas import tpu as pltpu
from jax.sharding import PartitionSpec as P

HD = 128
GROUP = 8
PAIR = 2
ROWS = 8
STEPS = 2
PAGE = 16
NZ = 8
QR = STEPS * GROUP
PIECE = 24
NEG = -1e30
MESH = pl.DeviceIdType.MESH
SCHEDULE = (((0, 3),), ((1, 3),), ((0, 3),), ((1, 3),), ((3, 3),), ((2, 3),), ((3, 1), (2, 1), (3, 1), (2, 1), (3, 1), (2, 1), (3, 1), (2, 1)), ((0, 1), (1, 1)))


TAIL_ORDER = (4, 1, 7, 3, 5, 2, 6)


def far_first(count):
    return sorted(range(1, count), key=lambda d: (-min(d, count - d), d))


def nt(a, b):
    return lax.dot_general(a, b, (((1,), (1,)), ((), ())), preferred_element_type=jnp.float32)


def nn(a, b):
    return jnp.dot(a, b, preferred_element_type=jnp.float32)


def body(
    ny, nkv, out_here, pages_here,
    ctx_len, tail_count, hidden, w_qkv, w_out, keys, values, selected, tail_k, tail_v, dest,
    mixed, got_k, got_v,
    hid_v, wq_v, wo_v, k_v, v_v, sel_v, dest_v, tk_v, tv_v,
    part, ra1, a2s, ra2, qsend, qbuf, bias, bsend, rb1, b2s, rb2, asend, abuf, attf, csend, rc,
    stage_k, stage_v, mid_k, mid_v, inv_v, inv_s,
    in_sem, send_sem, za_sem, ya_sem, zq_sem, yb_sem, zb_sem, yt_sem, kv_sem,
    tail_send, tail_recv, inv_sem,
):
    ctx = lax.axis_index("ctx")
    kv = lax.axis_index("kv")
    z = lax.div(ctx, ny)
    y = lax.rem(ctx, ny)
    n_ctx = NZ * ny
    score_scale = 1.0 / math.sqrt(HD)
    tokens = pages_here * PAGE
    tail_tokens = out_here * PAGE

    def z_peer(d):
        peer = lax.rem(z + d, NZ)
        return peer, (peer * ny + y, kv)

    def y_peer(d):
        peer = lax.rem(y + d, ny)
        return peer, (z * ny + peer, kv)

    def kv_peer(d):
        peer = lax.rem(kv + d, nkv)
        return peer, (ctx, peer)

    barrier = pltpu.get_barrier_semaphore()
    peers = NZ - 1 + ny - 1 + nkv - 1
    for count, peer_of in ((NZ, z_peer), (ny, y_peer), (nkv, kv_peer)):
        for d in far_first(count):
            pl.semaphore_signal(barrier, inc=1, device_id=peer_of(d)[1], device_id_type=MESH)

    first = lax.div(ctx * out_here, 128) * 128
    loads = [
        (hidden, hid_v),
        (w_qkv, wq_v),
        (dest.at[:, pl.ds(pl.multiple_of(first, 128), 128)], dest_v),
        (tail_k, tk_v.at[pl.ds(0, out_here)]),
        (tail_v, tv_v.at[pl.ds(0, out_here)]),
        (selected, sel_v),
        (keys, k_v),
        (values, v_v),
        (w_out, wo_v),
    ]
    loads = [pltpu.make_async_copy(a, b, in_sem.at[i]) for i, (a, b) in enumerate(loads)]
    for load in loads:
        load.start()

    loads[0].wait()
    loads[1].wait()
    proj = nn(hid_v[...], wq_v[...])
    for j in range(GROUP + 2):
        for s in range(STEPS):
            at = s * GROUP + j if j < GROUP else QR + (j - GROUP) * STEPS + s
            part[pl.ds(at, ROWS, stride=PIECE), :] = proj[s * ROWS:(s + 1) * ROWS, j * HD:(j + 1) * HD]

    tk_v[out_here] = jnp.zeros((PAGE, HD), jnp.bfloat16)
    tv_v[out_here] = jnp.zeros((PAGE, HD), jnp.bfloat16)
    loads[2].wait()
    offset = ctx * out_here - first
    sub = lax.broadcasted_iota(jnp.int32, (128, 128), 0)
    lane = lax.broadcasted_iota(jnp.int32, (128, 128), 1)
    lane_mine = (lane >= offset) & (lane < offset + out_here)
    sub_mine = (sub >= offset) & (sub < offset + out_here)
    dest_row = jnp.broadcast_to(dest_v[...], (128, 128))
    dest_col = jnp.sum(jnp.where(sub == lane, dest_row, 0), axis=1, keepdims=True)
    same = (dest_row == dest_col) & lane_mine & (lane < sub)
    rank_col = jnp.sum(jnp.where(same, 1, 0), axis=1, keepdims=True)
    target = dest_col * PAIR + rank_col
    hit = (lane == target) & sub_mine
    table = jnp.sum(jnp.where(hit, sub - offset - out_here, 0), axis=0, keepdims=True) + out_here
    inv_v[...] = jnp.broadcast_to(table, (8, 128))
    table_copy = pltpu.make_async_copy(inv_v, inv_s, inv_sem.at[0])
    table_copy.start()

    loads[3].wait()
    loads[4].wait()
    table_copy.wait()

    def place(d, carry):
        to_z = lax.div(d, ny)
        to_y = lax.rem(d, ny)
        for k in range(PAIR):
            page = inv_s[0, d * PAIR + k]
            stage_k[to_y, to_z, k] = tk_v[page]
            stage_v[to_z, to_y, k] = tv_v[page]
        return carry

    lax.fori_loop(0, n_ctx, place, 0)
    pl.semaphore_wait(barrier, peers)

    def piece(i):
        return pl.ds(pl.multiple_of(i * PIECE, 8), PIECE)

    def q_rows(i):
        return pl.ds(pl.multiple_of(i * QR, QR), QR)

    def exchange(phase, count, peer_of, me, src, dst, recv):
        copies = []
        for d in far_first(count):
            peer, device = peer_of(d)
            copy = pltpu.make_async_remote_copy(
                src_ref=src(peer), dst_ref=dst(me), send_sem=send_sem.at[phase, d], recv_sem=recv.at[me],
                device_id=device, device_id_type=MESH,
            )
            copy.start()
            copies.append(copy)

        def wait():
            for d in range(1, count):
                peer, device = peer_of(d)
                pltpu.make_async_remote_copy(
                    src_ref=src(peer), dst_ref=dst(peer), send_sem=send_sem.at[phase, d], recv_sem=recv.at[peer],
                    device_id=device, device_id_type=MESH,
                ).wait_recv()

        return wait, copies

    sent = []

    tail_peer = (y_peer, z_peer, z_peer, y_peer)
    tail_order = (TAIL_ORDER,) * 4
    tail_src = (
        lambda p: stage_k.at[p], lambda p: stage_v.at[p], lambda p: mid_k.at[:, p], lambda p: mid_v.at[:, p],
    )
    tail_dst = (mid_k.at[y], mid_v.at[z], got_k.at[z], got_v.at[:, y])
    tail_me = (y, z, z, y)
    landing = (mid_k, mid_v, got_k, got_v)
    begun = [0, 0, 0, 0]

    def tail_start(phase):
        for kind, number in SCHEDULE[phase]:
            if begun[kind] == 0:
                if kind >= 2:
                    pltpu.make_async_copy(landing[kind - 2], landing[kind - 2], tail_recv.at[kind - 2]).wait()
                pltpu.make_async_copy(tail_src[kind](tail_me[kind]), tail_dst[kind], tail_recv.at[kind]).start()
            for d in tail_order[kind][begun[kind]:begun[kind] + number]:
                peer, device = tail_peer[kind](d)
                pltpu.make_async_remote_copy(
                    src_ref=tail_src[kind](peer), dst_ref=tail_dst[kind], send_sem=tail_send.at[kind],
                    recv_sem=tail_recv.at[kind], device_id=device, device_id_type=MESH,
                ).start()
            begun[kind] += number

    wait, copies = exchange(0, NZ, z_peer, z, lambda p: part.at[piece(p)], lambda m: ra1.at[m], za_sem)
    sent += copies
    ra1[z] = part[piece(z), :]

    tail_start(0)

    wait()
    a2s[...] = functools.reduce(lambda a, b: a + b, [ra1[i] for i in range(NZ)])
    wait, copies = exchange(1, ny, y_peer, y, lambda p: a2s, lambda m: ra2.at[m], ya_sem)
    sent += copies
    ra2[y] = a2s[...]
    tail_start(1)

    loads[5].wait()
    token = lax.broadcasted_iota(jnp.int32, (1, tokens), 1)
    page = lax.shift_right_logical(token, 4)
    for r in range(ROWS):
        inside = ctx * tokens + token < ctx_len[r]
        for s in range(STEPS):
            rel = sel_v[s, r] - ctx * pages_here
            bit = lax.shift_left(jnp.ones_like(rel), jnp.bitwise_and(rel, 15)).astype(jnp.float32)
            low = jnp.sum(jnp.where((rel >= 0) & (rel < 16), bit, 0.0), axis=1, keepdims=True).astype(jnp.int32)
            high = jnp.sum(jnp.where((rel >= 16) & (rel < 32), bit, 0.0), axis=1, keepdims=True).astype(jnp.int32)
            word = jnp.where(page < 16, low, high)
            live = jnp.bitwise_and(lax.shift_right_logical(word, jnp.bitwise_and(page, 15)), 1) == 1
            bias[pl.ds(r * STEPS + s, 1), :] = jnp.where(live & inside, 0.0, NEG)

    wait()
    total = functools.reduce(lambda a, b: a + b, [ra2[i] for i in range(ny)])
    rounded = total.astype(jnp.bfloat16)
    my_q = rounded[:QR]
    new_kv = rounded.astype(jnp.float32)[QR:QR + 2 * STEPS]
    qsend[...] = my_q
    wait, copies = exchange(2, NZ, z_peer, z, lambda p: qsend, lambda m: qbuf.at[q_rows(m)], zq_sem)
    sent += copies
    qbuf[q_rows(z), :] = my_q
    tail_start(2)

    tail_token = lax.broadcasted_iota(jnp.int32, (1, tail_tokens), 1)
    slot = lax.shift_right_logical(tail_token, 4) + ctx * out_here
    tail_row = jnp.zeros((1, tail_tokens), jnp.int32)
    end = 0
    for r in range(ROWS):
        end = end + tail_count[r]
        tail_row = tail_row + jnp.where(slot >= end, 1, 0)
    loads[6].wait()
    loads[7].wait()
    wait()

    tail_start(7)
    q_all = qbuf[...]
    scores_t = nt(q_all, tk_v[pl.ds(0, out_here)].reshape(tail_tokens, HD)) * score_scale
    q_row = lax.shift_right_logical(lax.broadcasted_iota(jnp.int32, (ROWS * QR, tail_tokens), 0), 4)
    scores_t = jnp.where(q_row == tail_row, scores_t, NEG)
    peak_t = jnp.max(scores_t, axis=1, keepdims=True)
    scores_r, peaks = [], []
    for r in range(ROWS):
        masked = nt(q_all[r * QR:(r + 1) * QR], k_v[r]) * score_scale
        masked = jnp.concatenate([
            masked[s * GROUP:(s + 1) * GROUP] + bias[pl.ds(r * STEPS + s, 1), :] for s in range(STEPS)
        ], axis=0)
        scores_r.append(masked)
        peaks.append(jnp.maximum(jnp.max(masked, axis=1, keepdims=True), peak_t[r * QR:(r + 1) * QR]))
    weights_t = jnp.exp(scores_t - jnp.concatenate(peaks, axis=0))
    sums_t = jnp.sum(weights_t, axis=1, keepdims=True)
    out_t = nn(weights_t.astype(jnp.bfloat16), tv_v[pl.ds(0, out_here)].reshape(tail_tokens, HD))
    lanes = lax.broadcasted_iota(jnp.int32, (QR, HD), 1)

    def parts(v):
        high = v.astype(jnp.bfloat16).astype(jnp.float32)
        middle = (v - high).astype(jnp.bfloat16).astype(jnp.float32)
        return high, middle, v - high - middle

    def pack(m, l):
        tile = jnp.zeros((QR, HD), jnp.float32)
        for i, part_of in enumerate(parts(m) + parts(l)):
            tile = jnp.where(lanes == i, part_of, tile)
        return tile.astype(jnp.bfloat16)

    for r in range(ROWS):
        weights_r = jnp.exp(scores_r[r] - peaks[r])
        sums = jnp.sum(weights_r, axis=1, keepdims=True) + sums_t[r * QR:(r + 1) * QR]
        out_r = nn(weights_r.astype(jnp.bfloat16), v_v[r]) + out_t[r * QR:(r + 1) * QR]
        bsend[r, pl.ds(0, QR), :] = out_r.astype(jnp.bfloat16)
        bsend[r, pl.ds(QR, QR), :] = pack(peaks[r], sums)

    wait, copies = exchange(3, ny, y_peer, y, lambda p: bsend.at[p], lambda m: rb1.at[m], yb_sem)
    sent += copies
    rb1[y] = bsend[y]
    tail_start(3)

    q_f = my_q.astype(jnp.float32)
    own_scores = [
        jnp.sum(q_f * new_kv[u:u + 1], axis=1, keepdims=True) * score_scale for u in range(STEPS)
    ]
    step_of = lax.shift_right_logical(lax.broadcasted_iota(jnp.int32, (QR, 1), 0), 3)
    own_scores = [jnp.where((step_of >= u) & (z == y), own_scores[u], NEG) for u in range(STEPS)]

    def merge(ref, count):
        tiles = [ref[i, pl.ds(QR, QR), :].astype(jnp.float32) for i in range(count)]
        ms = [t[:, 0:1] + t[:, 1:2] + t[:, 2:3] for t in tiles]
        ls = [t[:, 3:4] + t[:, 4:5] + t[:, 5:6] for t in tiles]
        return ms, ls, [ref[i, pl.ds(0, QR), :].astype(jnp.float32) for i in range(count)]

    def combine(ms, ls, os, m):
        factors = [jnp.exp(a - m) for a in ms]
        l = functools.reduce(lambda a, b: a + b, [f * a for f, a in zip(factors, ls)])
        o = functools.reduce(lambda a, b: a + b, [f * a for f, a in zip(factors, os)])
        return m, l, o

    wait()
    ms, ls, os = merge(rb1, ny)
    peak = functools.reduce(jnp.maximum, ms + own_scores)
    own = [jnp.exp(a - peak) for a in own_scores]
    _, l, o = combine(ms, ls, os, peak)
    for u, w in enumerate(own):
        l = l + w
        o = o + w.astype(jnp.bfloat16).astype(jnp.float32) * new_kv[STEPS + u:STEPS + u + 1]
    b2s[pl.ds(0, QR), :] = o.astype(jnp.bfloat16)
    b2s[pl.ds(QR, QR), :] = pack(peak, l)
    wait, copies = exchange(4, NZ, z_peer, z, lambda p: b2s, lambda m: rb2.at[m], zb_sem)
    sent += copies
    rb2[z] = b2s[...]
    tail_start(4)
    wait()
    ms, ls, os = merge(rb2, NZ)
    _, l, o = combine(ms, ls, os, functools.reduce(jnp.maximum, ms))
    att = (o / l).astype(jnp.bfloat16)
    asend[...] = att
    wait, copies = exchange(5, ny, y_peer, y, lambda p: asend, lambda m: abuf.at[q_rows(m)], yt_sem)
    sent += copies
    abuf[q_rows(y), :] = att
    tail_start(5)
    loads[8].wait()
    wait()
    attf[...] = abuf[...].astype(jnp.float32)
    att_all = jnp.concatenate([
        jnp.concatenate([attf[pl.ds(s * GROUP + g, ROWS, stride=QR), :] for s in range(STEPS)], axis=0)
        for g in range(GROUP)
    ], axis=1).astype(jnp.bfloat16)
    mine = nn(att_all, wo_v[...])
    csend[...] = mine
    wait, copies = exchange(6, nkv, kv_peer, kv, lambda p: csend, lambda m: rc.at[m], kv_sem)
    sent += copies
    rc[kv] = mine
    tail_start(6)
    for copy in sent[:-len(copies)]:
        copy.wait_send()
    wait()
    mixed[...] = functools.reduce(lambda a, b: a + b, [rc[i] for i in range(nkv)]).astype(jnp.bfloat16)

    for copy in copies:
        copy.wait_send()
    for kind in (2, 3):
        pltpu.make_async_copy(landing[kind], landing[kind], tail_recv.at[kind]).wait()
    for kind, ref in enumerate((stage_k, stage_v, got_k, got_v)):
        others = ref.at[pl.ds(0, len(tail_order[kind]))]
        pltpu.make_async_copy(others, others, tail_send.at[kind]).wait()


def store_body(nz, rows, got_k, got_v, mixed, out_k, out_v, bounds, sem):
    mixed[...] = rows[...]
    copies = [
        pltpu.make_async_copy(got, out, sem.at[i]) for i, (got, out) in enumerate(((got_k, out_k), (got_v, out_v)))
    ]
    for copy in copies:
        copy.start()
    count = got_k.shape[1] * PAIR

    def step(i, carry):
        pages = got_k[i].astype(jnp.float32).reshape(count, PAGE, HD)
        at = pl.ds(pl.multiple_of(i * count, count), count)
        bounds[at] = jnp.stack([jnp.min(pages, axis=1), jnp.max(pages, axis=1)], axis=1).astype(jnp.bfloat16)
        return carry

    lax.fori_loop(0, nz, step, 0)
    for copy in copies:
        copy.wait()


def on_device(
    hidden, w_qkv, w_out, key_pages, value_pages, ctx_len, selected,
    tail_keys, tail_values, tail_count, tail_dest,
):
    n_ctx = lax.axis_size("ctx")
    nkv = lax.axis_size("kv")
    ny = n_ctx // NZ
    pages_here = key_pages.shape[1]
    out_here = tail_keys.shape[0]
    tokens = pages_here * PAGE
    tail_tokens = out_here * PAGE
    bf, f32, i32 = jnp.bfloat16, jnp.float32, jnp.int32
    any_spec = pl.BlockSpec(memory_space=pltpu.HBM)
    smem = pl.BlockSpec(memory_space=pltpu.SMEM)
    vmem = pl.BlockSpec(memory_space=pltpu.VMEM)
    dma = pltpu.SemaphoreType.DMA
    tail_shape = (NZ, ny, PAIR, PAGE, HD)
    turned = (ny, NZ, PAIR, PAGE, HD)
    rows, got_k, got_v = pl.pallas_call(
        functools.partial(body, ny, nkv, out_here, pages_here),
        out_shape=(
            pltpu.VMEM((STEPS * ROWS, HD), bf),
            pltpu.VMEM(tail_shape, bf),
            pltpu.VMEM(tail_shape, bf),
        ),
        in_specs=[smem, smem] + [any_spec] * 9,
        out_specs=(vmem, vmem, vmem),
        scratch_shapes=[
            pltpu.VMEM((STEPS * ROWS, HD), bf),
            pltpu.VMEM(w_qkv.shape, bf),
            pltpu.VMEM(w_out.shape, bf),
            pltpu.VMEM((ROWS, tokens, HD), bf),
            pltpu.VMEM((ROWS, tokens, HD), bf),
            pltpu.VMEM(selected.shape, i32),
            pltpu.VMEM((1, 128), i32),
            pltpu.VMEM((out_here + 1, PAGE, HD), bf),
            pltpu.VMEM((out_here + 1, PAGE, HD), bf),
            pltpu.VMEM((ROWS * PIECE, HD), f32),
            pltpu.VMEM((NZ, PIECE, HD), f32),
            pltpu.VMEM((PIECE, HD), f32),
            pltpu.VMEM((ny, PIECE, HD), f32),
            pltpu.VMEM((QR, HD), bf),
            pltpu.VMEM((ROWS * QR, HD), bf),
            pltpu.VMEM((ROWS * STEPS, tokens), f32),
            pltpu.VMEM((ROWS, 2 * QR, HD), bf),
            pltpu.VMEM((ny, 2 * QR, HD), bf),
            pltpu.VMEM((2 * QR, HD), bf),
            pltpu.VMEM((NZ, 2 * QR, HD), bf),
            pltpu.VMEM((QR, HD), bf),
            pltpu.VMEM((ROWS * QR, HD), bf),
            pltpu.VMEM((ROWS * QR, HD), f32),
            pltpu.VMEM((STEPS * ROWS, HD), f32),
            pltpu.VMEM((nkv, STEPS * ROWS, HD), f32),
            pltpu.VMEM(turned, bf),
            pltpu.VMEM(tail_shape, bf),
            pltpu.VMEM(turned, bf),
            pltpu.VMEM(tail_shape, bf),
            pltpu.VMEM((8, 128), i32),
            pltpu.SMEM((8, 128), i32),
            dma((9,)),
            dma((7, 8)),
            dma((NZ,)),
            dma((ny,)),
            dma((NZ,)),
            dma((ny,)),
            dma((NZ,)),
            dma((ny,)),
            dma((nkv,)),
            dma((4,)),
            dma((4,)),
            dma((1,)),
        ],
        compiler_params=pltpu.CompilerParams(
            collective_id=0, has_side_effects=True, vmem_limit_bytes=60 * 1024 * 1024
        ),
    )(
        ctx_len, tail_count, hidden.reshape(STEPS * ROWS, HD), w_qkv, w_out,
        key_pages.reshape(ROWS, tokens, HD), value_pages.reshape(ROWS, tokens, HD), selected,
        tail_keys, tail_values, tail_dest.T,
    )
    mixed, out_k, out_v, bounds = pl.pallas_call(
        functools.partial(store_body, NZ),
        out_shape=(
            jax.ShapeDtypeStruct((STEPS * ROWS, HD), bf),
            jax.ShapeDtypeStruct(tail_shape, bf),
            jax.ShapeDtypeStruct(tail_shape, bf),
            jax.ShapeDtypeStruct((n_ctx * PAIR, 2, HD), bf),
        ),
        in_specs=[vmem, vmem, vmem],
        out_specs=(vmem, any_spec, any_spec, vmem),
        scratch_shapes=[dma((2,))],
        compiler_params=pltpu.CompilerParams(vmem_limit_bytes=16 * 1024 * 1024),
    )(rows, got_k, got_v)
    return (
        mixed.reshape(STEPS, ROWS, HD),
        out_k.reshape(n_ctx * PAIR, PAGE, HD),
        out_v.reshape(n_ctx * PAIR, PAGE, HD),
        bounds,
    )


def solution(mesh):
    placed = (
        P(None, None, "ctx"),
        P("ctx", "kv"),
        P("kv", "ctx"),
        P(None, "ctx", None, "kv"),
        P(None, "ctx", None, "kv"),
        P(),
        P(None, None, "kv", None),
        P("ctx", None, "kv"),
        P("ctx", None, "kv"),
        P(),
        P(),
    )
    return jax.shard_map(
        on_device,
        mesh=mesh,
        in_specs=placed,
        out_specs=(
            P(None, None, "ctx"),
            P("ctx", None, "kv"),
            P("ctx", None, "kv"),
            P("ctx", None, "kv"),
        ),
        check_vma=False,
    )
```
